128 devices in a mesh: ctx: 16 (over y, z_lo, core), head: 8 (over x, z_hi).
Axes of the slice: x: 4, y: 4, z: 4 (z_hi: 2, z_lo: 2; z = z_hi * 2 + z_lo), core: 2. Of those that a mesh axis runs over, the one named last changes fastest.
Arguments:
- activations: bfloat16 [6144, 4096], P('ctx'), may hold values from -24 to 24
- noise_mask: int32 [6144], P('ctx'), may hold values 0 or 1
- span_order: int32 [32], replicated, may hold values from 0 to 31, each once
- mask_vector: bfloat16 [4096], replicated, may hold values from -6 to 6
- input_weights: bfloat16 [3, 4096, 4096], P(None, None, 'head'), may hold values from -0.09375 to 0.09375
- output_weight: bfloat16 [4096, 4096], P('head'), may hold values from -0.09375 to 0.09375
Outputs:
- mixed_out: bfloat16 [6144, 8192], P(('ctx', 'head'))
The draws below stay inside these ranges and needn't reach their ends.
Inputs may be any that keep to these rules, and one draw needn't show every extreme that they name: A permutation; slot s holds document tokens span_order[s] * (192) onward. `noise_mask`: 1 marks a token of the noisy copy replaced by mask_vector.
All inputs are finite; a program needn't handle non-finite values. No bound on the sum of `noise_mask` on one device may be relied on, other than what follows from the above.
Results may differ from the reference program's by a relative error of at most 0.019.
Values may be sent and summed in bfloat16 or wider, within the bound.
A program may use at most 128 MiB of HBM per device.

```python
import math
import jax
import jax.numpy as jnp
from jax import lax

D = 4096
HEADS = 32
HEAD_SIZE = 128
DOCUMENT_TOKENS = 384
DIFFUSION_TOKENS = 64
DOC = 6144
N_CTX = 16
N_HEAD = 8


def draw_activations(key, part):
    key = jax.random.fold_in(key, 7)
    base_key = jax.random.fold_in(key, 0)
    values = jnp.clip(jax.random.normal(base_key, (DOC, D), jnp.float32), -6.0, 6.0)
    return values.astype(jnp.bfloat16)


def place_ends(values, stream_key, least, top_value):
    shape = values.shape
    index_at = [jax.random.randint(jax.random.fold_in(stream_key, axis), (), 0, shape[axis]) for axis in range(len(shape))]
    values = values.at[tuple(index_at)].set(least)
    longest = shape.index(max(shape))
    index_at[longest] = (index_at[longest] + 1) % shape[longest]
    return values.at[tuple(index_at)].set(top_value)


def steps_of(own_key, dims, shards, least, largest):
    def one(axis_at, blocks):
        draws = jax.random.uniform(jax.random.fold_in(jax.random.fold_in(own_key, 6), axis_at), (blocks,), jnp.float32, least / len(shards), largest / len(shards))
        return jnp.repeat(jnp.exp(draws), dims[axis_at] // blocks).reshape((-1,) + (1,) * (len(dims) - axis_at - 1))

    factor_of = one(*shards[0])
    for cut in shards[1:]:
        factor_of = factor_of * one(*cut)
    return factor_of


def noise(rng, shape, width, reach, shards=(), held_as=jnp.bfloat16):
    loudness = steps_of(rng, shape, shards, -0.22, 0.18) if shards else 1.0
    drawn = jax.random.normal(rng, shape, jnp.float32) * width * loudness
    return jnp.minimum(jnp.maximum(drawn, -reach), reach).astype(held_as)


def setup_inputs(seed: int = 0) -> dict:
    seeds = jax.random.split(jax.random.key(seed), 7)
    activations = draw_activations(jax.random.fold_in(seeds[6], 71), 0)
    noise_mask = place_ends((jax.random.randint(seeds[1], (DOC,), 0, 2) < 1).astype(jnp.int32), jax.random.fold_in(seeds[1], 1), 0, 1)
    span_order = jax.random.permutation(seeds[2], 2 * N_CTX).astype(jnp.int32)
    mask_vector = noise(seeds[3], (D,), 1.0, 6.0)
    input_weights = noise(seeds[4], (3, D, HEADS * HEAD_SIZE), D ** -0.5, 0.09375, ((2, 8),))
    output_weight = noise(seeds[5], (HEADS * HEAD_SIZE, D), (HEADS * HEAD_SIZE) ** -0.5, 0.09375, ((0, 8),))
    return dict(activations=activations, noise_mask=noise_mask, span_order=span_order, mask_vector=mask_vector, input_weights=input_weights, output_weight=output_weight)


def slot_positions(span_order):
    half_rows = DOCUMENT_TOKENS // 2
    row_index = jnp.arange(DOC, dtype=jnp.int32)
    return (span_order[row_index // half_rows] * half_rows + row_index % half_rows).astype(jnp.int32)

def reference(activations, noise_mask, span_order, mask_vector, input_weights, output_weight):
    noisy_rows = jnp.where(noise_mask[:, None] == 1, mask_vector[None, :], activations)
    stacked = jnp.concatenate([activations, noisy_rows], axis=0)
    queries = jnp.dot(stacked, input_weights[0], preferred_element_type=jnp.float32).astype(jnp.bfloat16)
    key_rows = jnp.dot(stacked, input_weights[1], preferred_element_type=jnp.float32).astype(jnp.bfloat16)
    value_rows = jnp.dot(stacked, input_weights[2], preferred_element_type=jnp.float32).astype(jnp.bfloat16)
    key_blocks = slot_positions(span_order) // DIFFUSION_TOKENS
    logit_scale_factor = 1.0 / math.sqrt(HEAD_SIZE)

    def split_heads(matrix):
        return matrix.reshape(2 * DOC, HEADS, HEAD_SIZE).transpose(1, 0, 2)

    def head_output(inputs):
        head_q, head_k, head_v = inputs
        clean_keys = head_k[:DOC]
        clean_values = head_v[:DOC]
        noisy_keys = head_k[DOC:]
        noisy_values = head_v[DOC:]

        def clean_block(block_index):
            first_row = block_index * DOCUMENT_TOKENS
            block_queries = lax.dynamic_slice_in_dim(head_q, first_row, DOCUMENT_TOKENS, 0)
            query_blocks = lax.dynamic_slice_in_dim(key_blocks, first_row, DOCUMENT_TOKENS, 0)
            scores = jnp.dot(block_queries, clean_keys.T, preferred_element_type=jnp.float32) * logit_scale_factor
            allowed = key_blocks[None, :] <= query_blocks[:, None]
            scores = jnp.where(allowed, scores, jnp.float32(-1e+30))
            row_top = scores.max(axis=1, keepdims=True)
            weights = jnp.where(allowed, jnp.exp(scores - row_top), jnp.float32(0.0))
            row_total = weights.sum(axis=1, keepdims=True)
            return jnp.dot(weights.astype(jnp.bfloat16), clean_values, preferred_element_type=jnp.float32) / row_total

        def noisy_block(block_index):
            first_row = block_index * DOCUMENT_TOKENS
            block_queries = lax.dynamic_slice_in_dim(head_q, DOC + first_row, DOCUMENT_TOKENS, 0)
            query_blocks = lax.dynamic_slice_in_dim(key_blocks, first_row, DOCUMENT_TOKENS, 0)
            scores = jnp.dot(block_queries, clean_keys.T, preferred_element_type=jnp.float32) * logit_scale_factor
            allowed = key_blocks[None, :] < query_blocks[:, None]
            scores = jnp.where(allowed, scores, jnp.float32(-1e+30))
            grouped_query_rows = block_queries.astype(jnp.float32).reshape(-1, DIFFUSION_TOKENS, HEAD_SIZE)
            grouped_key_rows = lax.dynamic_slice_in_dim(noisy_keys, first_row, DOCUMENT_TOKENS, 0).astype(jnp.float32).reshape(-1, DIFFUSION_TOKENS, HEAD_SIZE)
            grouped_value_rows = lax.dynamic_slice_in_dim(noisy_values, first_row, DOCUMENT_TOKENS, 0).astype(jnp.float32).reshape(-1, DIFFUSION_TOKENS, HEAD_SIZE)
            self_block_scores = jnp.einsum('gxn,gsn->gxs', grouped_query_rows, grouped_key_rows, precision=lax.Precision.HIGHEST) * logit_scale_factor
            self_block_scores = self_block_scores.reshape(DOCUMENT_TOKENS, DIFFUSION_TOKENS)
            row_top = jnp.maximum(scores.max(axis=1), self_block_scores.max(axis=1))[:, None]
            weights = jnp.where(allowed, jnp.exp(scores - row_top), jnp.float32(0.0))
            own_weights = jnp.exp(self_block_scores - row_top)
            row_total = weights.sum(axis=1, keepdims=True) + own_weights.sum(axis=1, keepdims=True)
            rounded_result = lax.optimization_barrier(own_weights.astype(jnp.bfloat16)).astype(jnp.float32)
            self_block_output = jnp.einsum('urv,uvx->urx', rounded_result.reshape(-1, DIFFUSION_TOKENS, DIFFUSION_TOKENS), grouped_value_rows, precision=lax.Precision.HIGHEST).reshape(DOCUMENT_TOKENS, HEAD_SIZE)
            clean_part = jnp.dot(weights.astype(jnp.bfloat16), clean_values, preferred_element_type=jnp.float32)
            return (clean_part + self_block_output) / row_total
        block_list = jnp.arange(N_CTX, dtype=jnp.int32)
        clean_out = lax.map(clean_block, block_list).reshape(DOC, HEAD_SIZE)
        noisy_out = lax.map(noisy_block, block_list).reshape(DOC, HEAD_SIZE)
        return jnp.concatenate([clean_out, noisy_out], axis=0)
    outputs = lax.map(head_output, (split_heads(queries), split_heads(key_rows), split_heads(value_rows)))
    attended = outputs.transpose(1, 0, 2).reshape(2 * DOC, HEADS * HEAD_SIZE).astype(jnp.bfloat16)
    group_width = HEADS * HEAD_SIZE // N_HEAD

    def add_group(total, group_index):
        first_col = (group_index * group_width).astype(jnp.int32)
        columns = lax.dynamic_slice_in_dim(attended, first_col, group_width, 1)
        weight_rows = lax.dynamic_slice_in_dim(output_weight, first_col, group_width, 0)
        clean_proj = jnp.dot(columns[:DOC], weight_rows, preferred_element_type=jnp.float32)
        noisy_proj = jnp.dot(columns[DOC:], weight_rows, preferred_element_type=jnp.float32)
        partial_term = jnp.concatenate([clean_proj, noisy_proj], axis=1)
        rounded_term = lax.optimization_barrier(partial_term.astype(jnp.bfloat16)).astype(jnp.float32)
        return (total + rounded_term, None)
    start_total = jnp.zeros((DOC, 2 * D), jnp.float32)
    summed, _ = lax.scan(add_group, start_total, jnp.arange(N_HEAD, dtype=jnp.int32))
    return summed.astype(jnp.bfloat16)
```

```python
import functools
import math

import jax
import jax.numpy as jnp
from jax import lax
from jax.experimental import pallas as pl
from jax.experimental.pallas import tpu as pltpu
from jax.sharding import PartitionSpec as P

MESH = pl.DeviceIdType.MESH
HEAD = 128
ROWS = 384
HALF = 192
BLOCK = 64
QT = 208
NEG = -1e30
LOG2_SCALE = math.log2(math.e) / math.sqrt(HEAD)
F32 = jnp.float32
BF16 = jnp.bfloat16


def coords():
    i = lax.axis_index("ctx")
    j = lax.axis_index("head")
    return j // 2, i // 4, (i // 2) % 2, j % 2, i % 2


def ctx_of(y, zl, c):
    return (y * 2 + zl) * 2 + c


def rcopy(src, dst, ssem, rsem, dev):
    return pltpu.make_async_remote_copy(
        src_ref=src, dst_ref=dst, send_sem=ssem, recv_sem=rsem, device_id=dev, device_id_type=MESH
    )


def greet(devs):
    barrier = pltpu.get_barrier_semaphore()
    for dev in devs:
        pl.semaphore_signal(barrier, inc=1, device_id=dev, device_id_type=MESH)
    return lambda: pl.semaphore_wait(barrier, len(devs))


def project_kernel(
    act, nmask, mvec, w, wo,
    kv, q, mproj, msk, wq,
    lhs, wbuf, kvst, qst, lsem, wsem,
    y_s, y_r, q_s, q_r, m_s, m_r, z_s, c_s, f_r, x_s, x_r,
):
    x, y, zl, zh, c = coords()
    hd = lax.axis_index("head")
    me = ctx_of(y, zl, c)
    ydev = [(ctx_of(lax.rem(y + k, 4), zl, c), hd) for k in range(4)]
    zdev = (ctx_of(y, 1 - zl, c), hd)
    cdev = (ctx_of(y, zl, 1 - c), hd)
    xdev = (me, lax.rem(x + 2, 4) * 2 + zh)
    arrive = greet([ydev[1], ydev[2], ydev[3], zdev, cdev, xdev])

    act_in = pltpu.make_async_copy(act, lhs.at[pl.ds(0, ROWS)], lsem)
    act_in.start()
    order = (0, 1, 3, 2)
    win = []
    for n, k in enumerate(order):
        col = pl.multiple_of(lax.rem(y + k, 4) * HEAD, HEAD)
        group = []
        for part, m in enumerate((1, 2, 0)):
            cp = pltpu.make_async_copy(
                w.at[m, :, pl.ds(col, HEAD)],
                wbuf.at[n, :, pl.ds(part * HEAD, HEAD)],
                wsem.at[n, part],
            )
            cp.start()
            group.append(cp)
        win.append(group)
    lhs[pl.ds(ROWS, 16), :] = jnp.broadcast_to(mvec[...], (16, 4096))
    msk[y] = jnp.broadcast_to(nmask[...].astype(F32), (8, ROWS))
    act_in.wait()

    sends = []

    def start(cp):
        cp.start()
        sends.append(cp)

    qd = lax.rem(y, 2) * 2 + c
    qsends = []
    for n, k in enumerate(order):
        for cp in win[n]:
            cp.wait()
        if n == 0:
            r = jnp.dot(lhs[...], wbuf[0], preferred_element_type=F32)
            kv[me] = r[:ROWS, : 2 * HEAD].astype(BF16)
            q[y] = (r[:ROWS, 2 * HEAD :] * LOG2_SCALE).astype(BF16)
            mproj[:, : 2 * HEAD] = r[ROWS:, : 2 * HEAD].astype(BF16)
            mproj[:, 2 * HEAD :] = (r[ROWS:, 2 * HEAD :] * LOG2_SCALE).astype(BF16)
            arrive()
            start(rcopy(kv.at[me], kv.at[me], z_s.at[0], f_r.at[me], zdev))
            start(rcopy(kv.at[me], kv.at[me], c_s.at[0], f_r.at[me], cdev))
            qcol = pl.multiple_of(qd * 1024, 1024)
            start(rcopy(wo.at[:, pl.ds(qcol, 1024)], wq, x_s, x_r, xdev))
            for k2 in (1, 3, 2):
                start(rcopy(msk.at[y], msk.at[y], m_s.at[k2 - 1], m_r.at[y], ydev[k2]))
        else:
            r = jnp.dot(lhs[pl.ds(0, ROWS), :], wbuf[n], preferred_element_type=F32)
            kvst[n - 1] = r[:, : 2 * HEAD].astype(BF16)
            qst[n - 1] = (r[:, 2 * HEAD :] * LOG2_SCALE).astype(BF16)
            start(rcopy(kvst.at[n - 1], kv.at[me], y_s.at[n - 1], f_r.at[me], ydev[k]))
            qsends.append(rcopy(qst.at[n - 1], q.at[y], q_s.at[n - 1], q_r.at[y], ydev[k]))
    for cp in qsends:
        start(cp)

    def landed(slot):
        rcopy(kv.at[slot], kv.at[slot], z_s.at[0], f_r.at[slot], cdev).wait_recv()

    def from_y(n, k):
        slot = ctx_of(lax.rem(y + k, 4), zl, c)
        landed(slot)
        start(rcopy(kv.at[slot], kv.at[slot], z_s.at[n], f_r.at[slot], zdev))
        start(rcopy(kv.at[slot], kv.at[slot], c_s.at[n], f_r.at[slot], cdev))

    def from_z(n, k):
        slot = ctx_of(lax.rem(y + k, 4), 1 - zl, c)
        landed(slot)
        start(rcopy(kv.at[slot], kv.at[slot], c_s.at[4 + n], f_r.at[slot], cdev))

    from_y(1, 1)
    from_z(0, 0)
    from_y(2, 3)
    from_z(1, 1)
    from_y(3, 2)
    from_z(2, 3)
    from_z(3, 2)
    for k in order:
        for z2 in range(2):
            landed(ctx_of(lax.rem(y + k, 4), z2, 1 - c))
    for k in (1, 3, 2):
        yk = lax.rem(y + k, 4)
        rcopy(q.at[yk], q.at[yk], q_s.at[0], q_r.at[yk], cdev).wait_recv()
        rcopy(msk.at[yk], msk.at[yk], m_s.at[0], m_r.at[yk], cdev).wait_recv()
    rcopy(wo.at[:, pl.ds(0, 1024)], wq, x_s, x_r, xdev).wait_recv()
    for cp in sends:
        cp.wait_send()


def attend_kernel(span, kv, q, mproj, msk, keyspan, out, qt, vx, m_ref, o_ref):
    x, y, zl, zh, c = coords()
    p_x = x // 2
    ones = jnp.ones((ROWS, HEAD), BF16)
    for s in range(16):
        vx[pl.ds(s * ROWS, ROWS), pl.ds(0, HEAD)] = kv[s, :, HEAD:]
        vx[pl.ds(s * ROWS, ROWS), pl.ds(HEAD, HEAD)] = ones
    for s in range(4):
        for h in range(2):
            qt[2 * s + h, pl.ds(0, HALF), :] = q[s, pl.ds(h * HALF, HALF), :]
            qt[2 * s + h, pl.ds(HALF, 16), :] = mproj[:, 2 * HEAD :]
    km = mproj[:, :HEAD]
    vm = mproj[pl.ds(0, 1), pl.ds(HEAD, HEAD)].astype(F32)
    vm = jnp.concatenate([vm, jnp.ones((1, HEAD), F32)], axis=1)

    rowi = lax.broadcasted_iota(jnp.int32, (QT, HALF), 0)
    coli = lax.broadcasted_iota(jnp.int32, (QT, HALF), 1)
    bi = jnp.where(rowi < HALF, rowi // BLOCK, jnp.minimum(rowi - HALF, 2))
    bj = coli // BLOCK

    def one(i, _):
        s = i // 2
        h = lax.rem(i, 2)
        src = ctx_of(s, zl, c)
        u = span[2 * src + h]
        qi = qt[i]
        m_ref[...] = jnp.full((QT, HEAD), NEG, F32)
        o_ref[...] = jnp.zeros((QT, 2 * HEAD), F32)

        def keys(g, _):
            k = kv[pl.ds(4 * g, 4), :, :HEAD].reshape(4 * ROWS, HEAD)
            sc = lax.dot_general(qi, k, (((1,), (1,)), ((), ())), preferred_element_type=F32)
            ks = keyspan[g]
            sc = sc + jnp.where(ks < u, F32(0), F32(NEG))
            old = m_ref[:, :1]
            new = jnp.maximum(old, jnp.max(sc, axis=1, keepdims=True))
            p = jnp.exp2(sc - new).astype(BF16)
            start_row = pl.multiple_of(g * 4 * ROWS, 4 * ROWS)
            pv = jnp.dot(p, vx[pl.ds(start_row, 4 * ROWS), :], preferred_element_type=F32)
            o_ref[...] = o_ref[...] * jnp.exp2(old - new) + pv
            m_ref[...] = jnp.broadcast_to(new, (QT, HEAD))
            return 0

        lax.fori_loop(0, 4, keys, 0)

        row0 = pl.multiple_of(h * HALF, HALF)
        ko = kv[src, pl.ds(row0, HALF), :HEAD]
        vstart = pl.multiple_of(src * ROWS + h * HALF, HALF)
        vo = vx[pl.ds(vstart, HALF), :]
        so = lax.dot_general(qi, ko, (((1,), (1,)), ((), ())), preferred_element_type=F32)
        sm = lax.dot_general(qi, km, (((1,), (1,)), ((), ())), preferred_element_type=F32)[:, :1]
        mrow = jnp.where(h == 0, msk[s, pl.ds(0, 1), pl.ds(0, HALF)], msk[s, pl.ds(0, 1), pl.ds(HALF, HALF)])
        mp = m_ref[:, :1]
        op = o_ref[...]

        sc = jnp.where(bj <= bi, so, F32(NEG))
        mc = jnp.maximum(mp, jnp.max(sc, axis=1, keepdims=True))
        pc = jnp.where(bj <= bi, jnp.exp2(sc - mc), F32(0)).astype(BF16)
        oc = op * jnp.exp2(mp - mc) + jnp.dot(pc, vo, preferred_element_type=F32)
        clean = (oc[:HALF, :HEAD] / oc[:HALF, HEAD:]).astype(BF16)

        hit = (bj == bi) & (mrow > 0.5)
        sn = jnp.where(hit, sm, sc)
        mn = jnp.maximum(mp, jnp.max(sn, axis=1, keepdims=True))
        pn = jnp.where(bj <= bi, jnp.exp2(sn - mn), F32(0)).astype(BF16)
        pz = jnp.where(hit, F32(0), pn.astype(F32))
        wm = jnp.sum(pn.astype(F32) - pz, axis=1, keepdims=True)
        on = op * jnp.exp2(mp - mn) + jnp.dot(pz.astype(BF16), vo, preferred_element_type=F32) + wm * vm
        an = on[:, :HEAD] / on[:, HEAD:]
        mcol = jnp.sum(jnp.where(rowi == coli, mrow, F32(0)), axis=1, keepdims=True)[:HALF]
        masked = jnp.concatenate(
            [jnp.broadcast_to(an[HALF + b : HALF + b + 1], (BLOCK, HEAD)) for b in range(3)], axis=0
        )
        noisy = jnp.where(mcol > 0.5, masked, an[:HALF]).astype(BF16)

        for b in range(4):
            xo = 2 * h + b // 2
            zo = b % 2
            near = (zo == p_x)
            side = jnp.where(near, lax.rem(x + 1, 4), lax.rem(x + 3, 4))
            pos = jnp.where(
                xo == x,
                zo,
                jnp.where(
                    xo == lax.rem(x + 2, 4),
                    4 + zo,
                    jnp.where(near, 0, 4) + jnp.where(xo == side, 2, 3),
                ),
            )
            out[s, pos, pl.ds(0, 48), :] = clean[b * 48 : (b + 1) * 48]
            out[s, pos, pl.ds(48, 48), :] = noisy[b * 48 : (b + 1) * 48]
        return 0

    lax.fori_loop(0, 8, one, 0)


def mix_kernel(
    att, wo, wq, out,
    abuf, wown, wp, keep, xs, xr, zs, zr,
    l_sem, o_sem, a_s, a_r, wq_l, wc_s, wc_r, wy_s, wy_r, wf_s, wf_r, x_s, x_r, z_s, z_r,
):
    x, y, zl, zh, c = coords()
    hd = lax.axis_index("head")
    me = ctx_of(y, zl, c)
    x2 = lax.rem(x + 2, 4)
    adev = {}
    for t, xt in ((0, x), (1, x2)):
        for k in range(4):
            adev[t, k] = (ctx_of(lax.rem(y + k, 4), zl, c), xt * 2 + zh)
    cdev = (ctx_of(y, zl, 1 - c), hd)
    xup = (me, lax.rem(x + 1, 4) * 2 + zh)
    xdn = (me, lax.rem(x + 3, 4) * 2 + zh)
    zdev = (me, x * 2 + 1 - zh)
    wyk = lax.rem(y + 1 + 2 * c, 4)
    wydev = (ctx_of(wyk, zl, c), hd)
    arrive = greet([adev[t, k] for t in range(2) for k in range(4) if (t, k) != (0, 0)] + [cdev, xup, xdn, zdev])

    qd = lax.rem(y, 2) * 2 + c
    order = (qd, qd + 1 - 2 * c, lax.rem(qd + 2, 4), lax.rem(qd + 2, 4) + 1 - 2 * c)
    lcopy = []
    own_col = pl.multiple_of(y * HEAD, HEAD)
    cp = pltpu.make_async_copy(att.at[y, pl.ds(0, 4)], abuf.at[:, :, pl.ds(own_col, HEAD)], l_sem)
    cp.start()
    lcopy.append(cp)
    wl = []
    for n in range(4):
        col = pl.multiple_of(order[n] * 1024, 1024)
        cp = pltpu.make_async_copy(wo.at[:, pl.ds(col, 1024)], wown.at[n], o_sem.at[n])
        cp.start()
        wl.append(cp)
    wpl = pltpu.make_async_copy(wq, wp.at[0], wq_l)
    wpl.start()
    arrive()
    sends = []

    def start(cp):
        cp.start()
        sends.append(cp)

    for n, (t, k) in enumerate([(0, 2), (1, 2), (0, 1), (0, 3), (1, 1), (1, 3), (1, 0)]):
        yk = lax.rem(y + k, 4)
        dcol = pl.multiple_of((4 * t + y) * HEAD, HEAD)
        start(
            rcopy(
                att.at[yk, pl.ds(4 * t, 4)],
                abuf.at[:, :, pl.ds(dcol, HEAD)],
                a_s.at[n],
                a_r.at[4 * t + y],
                adev[t, k],
            )
        )
    wpl.wait()
    start(rcopy(wp.at[0], wp.at[1], wc_s, wc_r, cdev))
    for t, k in [(0, 1), (0, 3), (1, 0), (0, 2), (1, 1), (1, 3), (1, 2)]:
        yk = lax.rem(y + k, 4)
        dcol = pl.multiple_of((4 * t + yk) * HEAD, HEAD)
        rcopy(
            att.at[0, pl.ds(0, 4)], abuf.at[:, :, pl.ds(dcol, HEAD)], a_s.at[0], a_r.at[4 * t + yk], cdev
        ).wait_recv()
    for e in range(2):
        src = wp.at[0, :, pl.ds(e * 512, 512)]
        start(rcopy(src, wp.at[2, :, pl.ds(e * 512, 512)], wy_s.at[e], wy_r.at[e], wydev))
    for cp in lcopy:
        cp.wait()

    def matmul(n):
        j, e = n // 2, n % 2
        if e == 0:
            wl[j].wait()
        cols = pl.ds(e * 512, 512)
        if j == 1 and e == 0:
            rcopy(wp.at[0], wp.at[1], wc_s, wc_r, cdev).wait_recv()
        if j == 2:
            half = wp.at[2, :, cols]
            rcopy(half, half, wy_s.at[e], wy_r.at[e], cdev).wait_recv()
            start(rcopy(half, wp.at[3, :, cols], wf_s.at[e], wf_r.at[e], cdev))
        if j == 3:
            half = wp.at[3, :, cols]
            rcopy(half, half, wf_s.at[e], wf_r.at[e], cdev).wait_recv()
        a = abuf[...].reshape(ROWS, 1024)
        r = jnp.dot(a[:, :512], wown[j, :, cols], preferred_element_type=F32)
        r = r + jnp.dot(a[:, 512:], wp[j, :, cols], preferred_element_type=F32)
        keep[n] = r[:192].reshape(2, 96, 512)
        xs[n, 0] = r[192:288].astype(BF16)
        xs[n, 1] = r[288:].astype(BF16)
        start(rcopy(xs.at[n, 0], xr.at[n, 0], x_s.at[n, 0], x_r.at[n, 0], xup))
        start(rcopy(xs.at[n, 1], xr.at[n, 1], x_s.at[n, 1], x_r.at[n, 1], xdn))

    from_below = lax.rem(x + 3, 4) // 2

    def reduce_x(n):
        for d in range(2):
            rcopy(xs.at[n, d], xr.at[n, d], x_s.at[n, d], x_r.at[n, d], xup).wait_recv()
        far = 1 - zh
        keep[n, zh] = keep[n, zh] + xr[n, (zh + from_below) % 2].astype(F32)
        zs[n] = (keep[n, far] + xr[n, (far + from_below) % 2].astype(F32)).astype(BF16)
        start(rcopy(zs.at[n], zr.at[n], z_s.at[n], z_r.at[n], zdev))

    def reduce_z(n):
        rcopy(zs.at[n], zr.at[n], z_s.at[n], z_r.at[n], zdev).wait_recv()
        total = (keep[n, zh] + zr[n].astype(F32)).astype(BF16)
        col = pl.multiple_of(order[n // 2] * 1024 + (n % 2) * 512, 512)
        out[:, pl.ds(col, 512)] = total[:48]
        out[:, pl.ds(4096 + col, 512)] = total[48:]

    for n in range(4):
        matmul(n)
    reduce_x(0)
    reduce_x(1)
    matmul(4)
    reduce_x(2)
    matmul(5)
    reduce_z(0)
    reduce_x(3)
    matmul(6)
    reduce_z(1)
    reduce_x(4)
    matmul(7)
    reduce_z(2)
    reduce_x(5)
    reduce_z(3)
    reduce_x(6)
    reduce_z(4)
    reduce_x(7)
    for n in (5, 6, 7):
        reduce_z(n)
    for cp in sends:
        cp.wait_send()


def vmem():
    return pl.BlockSpec(memory_space=pltpu.VMEM)


def anyspace():
    return pl.BlockSpec(memory_space=pl.ANY)


def shards(activations, noise_mask, span_order, mask_vector, input_weights, output_weight):
    dma = pltpu.SemaphoreType.DMA
    params = functools.partial(pltpu.CompilerParams, has_side_effects=True, vmem_limit_bytes=56 << 20)
    kv, q, mproj, msk, wq = pl.pallas_call(
        project_kernel,
        out_shape=(
            jax.ShapeDtypeStruct((16, ROWS, 2 * HEAD), BF16),
            jax.ShapeDtypeStruct((4, ROWS, HEAD), BF16),
            jax.ShapeDtypeStruct((16, 3 * HEAD), BF16),
            jax.ShapeDtypeStruct((4, 8, ROWS), F32),
            jax.ShapeDtypeStruct((512, 1024), BF16),
        ),
        in_specs=[anyspace(), vmem(), vmem(), anyspace(), anyspace()],
        out_specs=(vmem(), vmem(), vmem(), vmem(), anyspace()),
        scratch_shapes=[
            pltpu.VMEM((ROWS + 16, 4096), BF16),
            pltpu.VMEM((4, 4096, 3 * HEAD), BF16),
            pltpu.VMEM((3, ROWS, 2 * HEAD), BF16),
            pltpu.VMEM((3, ROWS, HEAD), BF16),
            dma,
            dma((4, 3)),
            dma((3,)),
            dma((16,)),
            dma((3,)),
            dma((4,)),
            dma((3,)),
            dma((4,)),
            dma((4,)),
            dma((8,)),
            dma((16,)),
            dma,
            dma,
        ],
        compiler_params=params(collective_id=1),
        name="project",
    )(
        activations,
        noise_mask.reshape(1, ROWS),
        mask_vector.reshape(1, 4096),
        input_weights,
        output_weight,
    )
    keyspan = jnp.repeat(span_order, HALF).reshape(4, 1, 4 * ROWS)
    att = pl.pallas_call(
        attend_kernel,
        out_shape=jax.ShapeDtypeStruct((4, 8, 96, HEAD), BF16),
        in_specs=[pl.BlockSpec(memory_space=pltpu.SMEM)] + [vmem()] * 5,
        out_specs=vmem(),
        scratch_shapes=[
            pltpu.VMEM((8, QT, HEAD), BF16),
            pltpu.VMEM((16 * ROWS, 2 * HEAD), BF16),
            pltpu.VMEM((QT, HEAD), F32),
            pltpu.VMEM((QT, 2 * HEAD), F32),
        ],
        compiler_params=pltpu.CompilerParams(vmem_limit_bytes=48 << 20),
        name="attend",
    )(span_order, kv, q, mproj, msk, keyspan)
    return pl.pallas_call(
        mix_kernel,
        out_shape=jax.ShapeDtypeStruct((48, 8192), BF16),
        in_specs=[vmem(), anyspace(), anyspace()],
        out_specs=vmem(),
        scratch_shapes=[
            pltpu.VMEM((4, 96, 1024), BF16),
            pltpu.VMEM((4, 512, 1024), BF16),
            pltpu.VMEM((4, 512, 1024), BF16),
            pltpu.VMEM((8, 2, 96, 512), F32),
            pltpu.VMEM((8, 2, 96, 512), BF16),
            pltpu.VMEM((8, 2, 96, 512), BF16),
            pltpu.VMEM((8, 96, 512), BF16),
            pltpu.VMEM((8, 96, 512), BF16),
            dma,
            dma((4,)),
            dma((7,)),
            dma((8,)),
            dma,
            dma,
            dma,
            dma((2,)),
            dma((2,)),
            dma((2,)),
            dma((2,)),
            dma((8, 2)),
            dma((8, 2)),
            dma((8,)),
            dma((8,)),
        ],
        compiler_params=params(collective_id=2),
        name="mix",
    )(att, output_weight, wq)


def solution(mesh):
    in_specs = (P("ctx", None), P("ctx"), P(), P(), P(None, None, "head"), P("head", None))
    out_specs = P(("ctx", "head"), None)
    return jax.shard_map(shards, mesh=mesh, in_specs=in_specs, out_specs=out_specs, check_vma=False)
```

```python
import functools
import math

import jax
import jax.numpy as jnp
from jax import lax
from jax.experimental import pallas as pl
from jax.experimental.pallas import tpu as pltpu
from jax.sharding import PartitionSpec as P

MESH = pl.DeviceIdType.MESH
HEAD = 128
ROWS = 384
HALF = 192
BLOCK = 64
QT = 208
NEG = -1e30
VMEM_BYTES = 60 << 20
LOG2_SCALE = math.log2(math.e) / math.sqrt(HEAD)
F32 = jnp.float32
BF16 = jnp.bfloat16


def coords():
    i = lax.axis_index("ctx")
    j = lax.axis_index("head")
    return j // 2, i // 4, (i // 2) % 2, j % 2, i % 2


def ctx_of(y, zl, c):
    return (y * 2 + zl) * 2 + c


def rcopy(src, dst, ssem, rsem, dev):
    return pltpu.make_async_remote_copy(
        src_ref=src, dst_ref=dst, send_sem=ssem, recv_sem=rsem, device_id=dev, device_id_type=MESH
    )


def greet(devs):
    barrier = pltpu.get_barrier_semaphore()
    for dev in devs:
        pl.semaphore_signal(barrier, inc=1, device_id=dev, device_id_type=MESH)
    return lambda: pl.semaphore_wait(barrier, len(devs))


def kernel(
    span, act, nmask, mvec, w, wo, out,
    lhs, wbuf, st, kv, q, msk, qt, m_ref, o_ref, att, abuf, wown, wp, keep, xs, xr, zs, zr,
    act_l, w_l, wo_l, own_l, f_s, f_r, g_r, q_s, q_r, m_s, m_r, zk_s, zf_s, c_s, a_s, a_r,
    wx_s, wx_r, wc_s, wc_r, wy_s, wy_r, wf_s, wf_r, x_s, x_r, z_s, z_r,
):
    x, y, zl, zh, c = coords()
    hd = lax.axis_index("head")
    me = ctx_of(y, zl, c)
    ys = [y] + [lax.rem(y + k, 4) for k in (1, 2, 3)]
    x2 = lax.rem(x + 2, 4)
    ydev = [(ctx_of(ys[k], zl, c), hd) for k in range(4)]
    adev = [ydev, [(ctx_of(ys[k], zl, c), x2 * 2 + zh) for k in range(4)]]
    zdev = (ctx_of(y, 1 - zl, c), hd)
    ddev = (ctx_of(ys[2], 1 - zl, c), hd)
    cdev = (ctx_of(y, zl, 1 - c), hd)
    xup = (me, lax.rem(x + 1, 4) * 2 + zh)
    xdn = (me, lax.rem(x + 3, 4) * 2 + zh)
    hdev = (me, x * 2 + 1 - zh)
    wydev = (ctx_of(lax.rem(y + 1 + 2 * c, 4), zl, c), hd)
    arrive = greet(ydev[1:] + adev[1] + [zdev, ddev, cdev, xup, xdn, hdev])

    sends = []

    def start(cp):
        cp.start()
        sends.append(cp)

    loads = []
    for kc in range(4):
        part = pl.ds(kc * 1024, 1024)
        pair = (
            pltpu.make_async_copy(act.at[:, part], lhs.at[pl.ds(0, ROWS), part], act_l.at[kc]),
            pltpu.make_async_copy(w.at[0, part], wbuf.at[0, part], w_l.at[kc]),
        )
        for cp in pair:
            cp.start()
        loads.append(pair)
    wk = pltpu.make_async_copy(w.at[1], wbuf.at[1], w_l.at[4])
    wv = pltpu.make_async_copy(w.at[2], wbuf.at[2], w_l.at[5])
    wk.start()
    wv.start()
    qd = lax.rem(y, 2) * 2 + c
    order = (qd, qd + 1 - 2 * c, lax.rem(qd + 2, 4), lax.rem(qd + 2, 4) + 1 - 2 * c)
    wol = []
    for n in range(4):
        col = pl.multiple_of(order[n] * 1024, 1024)
        cp = pltpu.make_async_copy(wo.at[:, pl.ds(col, 1024)], wown.at[n], wo_l.at[n])
        cp.start()
        wol.append(cp)
    lhs[pl.ds(ROWS, 16), :] = jnp.broadcast_to(mvec[...], (16, 4096))
    msk[y] = jnp.broadcast_to(nmask[...].astype(F32), (8, ROWS))

    def keep_heads(m, r):
        for j in range(4):
            st[m, j] = r[:, j * HEAD : (j + 1) * HEAD].astype(BF16)

    rows = pl.ds(0, ROWS)
    r = None
    for kc in range(4):
        for cp in loads[kc]:
            cp.wait()
        part = pl.ds(kc * 1024, 1024)
        d = jnp.dot(lhs[:, part], wbuf[0, part], preferred_element_type=F32)
        r = d if r is None else r + d
    keep_heads(0, r * LOG2_SCALE)
    arrive()
    for k in (1, 3, 2):
        start(rcopy(st.at[0, ys[k], rows], q.at[y], q_s.at[k], q_r.at[y], ydev[k]))
        start(rcopy(msk.at[y], msk.at[y], m_s.at[k], m_r.at[y], ydev[k]))
    q[y] = st[0, y, rows]

    for m, cp in ((1, wk), (2, wv)):
        cp.wait()
        keep_heads(m, jnp.dot(lhs[...], wbuf[m], preferred_element_type=F32))
        dst = kv.at[me, m - 1]
        start(rcopy(st.at[m, y, rows], dst, zk_s.at[m - 1], f_r.at[m - 1, me], zdev))
        for k in (1, 3):
            start(rcopy(st.at[m, ys[k], rows], dst, f_s.at[m - 1, k], f_r.at[m - 1, me], ydev[k]))
        kv[me, m - 1] = st[m, y, rows]
    start(rcopy(kv.at[me], kv.at[me], c_s.at[0], g_r.at[me], cdev))
    for m in (1, 2):
        dst = kv.at[me, m - 1]
        start(rcopy(st.at[m, ys[2], rows], dst, f_s.at[m - 1, 2], f_r.at[m - 1, me], ydev[2]))
        start(rcopy(st.at[m, ys[2], rows], dst, f_s.at[m - 1, 0], f_r.at[m - 1, me], ddev))
    for e in range(2):
        col = pl.multiple_of(qd * 1024 + e * 512, 512)
        half = wp.at[0, :, pl.ds(e * 512, 512)]
        start(rcopy(wo.at[:, pl.ds(col, 512)], half, wx_s.at[e], wx_r.at[e], adev[1][0]))

    def here(k, z, split):
        slot = ctx_of(ys[k], z, c)
        if split:
            for m in range(2):
                rcopy(kv.at[slot, m], kv.at[slot, m], zk_s.at[m], f_r.at[m, slot], cdev).wait_recv()
        else:
            rcopy(kv.at[slot], kv.at[slot], zk_s.at[0], g_r.at[slot], cdev).wait_recv()
        return slot

    def to_core(n, slot):
        start(rcopy(kv.at[slot], kv.at[slot], c_s.at[n], g_r.at[slot], cdev))

    def to_z(n, slot):
        start(rcopy(kv.at[slot], kv.at[slot], zf_s.at[n], g_r.at[slot], zdev))

    def from_core(k, z):
        slot = ctx_of(ys[k], z, 1 - c)
        rcopy(kv.at[slot], kv.at[slot], zk_s.at[0], g_r.at[slot], cdev).wait_recv()

    def send_wp(e):
        half = wp.at[0, :, pl.ds(e * 512, 512)]
        rcopy(half, half, wx_s.at[e], wx_r.at[e], cdev).wait_recv()
        start(rcopy(half, wp.at[1, :, pl.ds(e * 512, 512)], wc_s.at[e], wc_r.at[e], cdev))
        start(rcopy(half, wp.at[2, :, pl.ds(e * 512, 512)], wy_s.at[e], wy_r.at[e], wydev))

    def chunk(pa, pb):
        place = lax.broadcasted_iota(jnp.int32, (1, 4 * ROWS), 1) // HALF
        ks = jnp.zeros((1, 4 * ROWS), jnp.int32)
        for n in range(8):
            ks = jnp.where(place == n, span[4 * (pa if n < 4 else pb) + n % 4], ks)
        refs = [(p, m) for m in range(2) for p in (pa, pb)]
        got = [kv[pl.ds(2 * p, 2), m].reshape(2 * ROWS, HEAD) for p, m in refs]
        k = jnp.concatenate(got[:2], axis=0)
        v = jnp.concatenate(got[2:], axis=0)
        return k, jnp.concatenate([v, jnp.ones((4 * ROWS, HEAD), BF16)], axis=1), ks

    def attend(i, u, keys, first):
        k, v, ks = keys
        sc = lax.dot_general(qt[i], k, (((1,), (1,)), ((), ())), preferred_element_type=F32)
        sc = sc + jnp.where(ks < u, F32(0), F32(NEG))
        top = jnp.max(sc, axis=1, keepdims=True)
        if first:
            new = jnp.maximum(top, F32(NEG))
        else:
            old = m_ref[i][:, :1]
            new = jnp.maximum(old, top)
        p = jnp.exp2(sc - new).astype(BF16)
        o = jnp.dot(p, v, preferred_element_type=F32)
        if not first:
            o = o_ref[i] * jnp.exp2(old - new) + o
        return new, o

    def step(pa, pb, first):
        keys = chunk(pa, pb)
        for i in range(8):
            u = span[2 * ctx_of(i // 2, zl, c) + i % 2]
            new, o = attend(i, u, keys, first)
            m_ref[i] = jnp.broadcast_to(new, (QT, HEAD))
            o_ref[i] = o

    def pair(k, z):
        return ys[k] * 2 + z

    to_core(1, here(0, 1 - zl, True))
    for n, k in ((0, 1), (1, 3)):
        slot = here(k, zl, True)
        to_z(n, slot)
        to_core(2 + n, slot)
    for k in (1, 3, 2):
        rcopy(q.at[ys[k]], q.at[ys[k]], q_s.at[1], q_r.at[ys[k]], cdev).wait_recv()
        rcopy(msk.at[ys[k]], msk.at[ys[k]], m_s.at[1], m_r.at[ys[k]], cdev).wait_recv()
    for s in range(4):
        for h in range(2):
            qt[2 * s + h, pl.ds(0, HALF), :] = q[s, pl.ds(h * HALF, HALF), :]
            qt[2 * s + h, pl.ds(HALF, 16), :] = st[0, y, pl.ds(ROWS, 16), :]
    from_core(0, zl)
    from_core(0, 1 - zl)
    step(pair(0, zl), pair(0, 1 - zl), True)
    from_core(1, zl)
    from_core(3, zl)
    step(pair(1, zl), pair(3, zl), False)
    to_core(4, here(2, zl, True))
    to_core(5, here(1, 1 - zl, False))
    send_wp(0)
    from_core(2, zl)
    from_core(1, 1 - zl)
    step(pair(2, zl), pair(1, 1 - zl), False)
    to_core(6, here(3, 1 - zl, False))
    to_core(7, here(2, 1 - zl, True))
    send_wp(1)
    from_core(3, 1 - zl)
    from_core(2, 1 - zl)

    p_x = x // 2
    km = st[1, y, pl.ds(ROWS, 16), :]
    vm = st[2, y, pl.ds(ROWS, 16), :][:1].astype(F32)
    vm = jnp.concatenate([vm, jnp.ones((1, HEAD), F32)], axis=1)
    rowi = lax.broadcasted_iota(jnp.int32, (QT, HALF), 0)
    coli = lax.broadcasted_iota(jnp.int32, (QT, HALF), 1)
    bi = jnp.where(rowi < HALF, rowi // BLOCK, jnp.minimum(rowi - HALF, 2))
    bj = coli // BLOCK
    last = chunk(pair(3, 1 - zl), pair(2, 1 - zl))

    def finish(s, h):
        i = 2 * s + h
        src = ctx_of(s, zl, c)
        mp, op = attend(i, span[2 * src + h], last, False)
        qi = qt[i]
        ko = kv[src, 0, pl.ds(h * HALF, HALF), :]
        vo = jnp.concatenate([kv[src, 1, pl.ds(h * HALF, HALF), :], jnp.ones((HALF, HEAD), BF16)], axis=1)
        so = lax.dot_general(qi, ko, (((1,), (1,)), ((), ())), preferred_element_type=F32)
        sm = lax.dot_general(qi, km, (((1,), (1,)), ((), ())), preferred_element_type=F32)[:, :1]
        mrow = msk[s, pl.ds(0, 1), pl.ds(h * HALF, HALF)]

        sc = jnp.where(bj <= bi, so, F32(NEG))
        mc = jnp.maximum(mp, jnp.max(sc, axis=1, keepdims=True))
        pc = jnp.where(bj <= bi, jnp.exp2(sc - mc), F32(0)).astype(BF16)
        oc = op * jnp.exp2(mp - mc) + jnp.dot(pc, vo, preferred_element_type=F32)
        clean = (oc[:HALF, :HEAD] / oc[:HALF, HEAD:]).astype(BF16)

        hit = (bj == bi) & (mrow > 0.5)
        sn = jnp.where(hit, sm, sc)
        mn = jnp.maximum(mp, jnp.max(sn, axis=1, keepdims=True))
        pn = jnp.where(bj <= bi, jnp.exp2(sn - mn), F32(0)).astype(BF16)
        pz = jnp.where(hit, F32(0), pn.astype(F32))
        wm = jnp.sum(pn.astype(F32) - pz, axis=1, keepdims=True)
        on = op * jnp.exp2(mp - mn) + jnp.dot(pz.astype(BF16), vo, preferred_element_type=F32) + wm * vm
        an = on[:, :HEAD] / on[:, HEAD:]
        mcol = jnp.sum(jnp.where(rowi == coli, mrow, F32(0)), axis=1, keepdims=True)[:HALF]
        masked = jnp.concatenate(
            [jnp.broadcast_to(an[HALF + b : HALF + b + 1], (BLOCK, HEAD)) for b in range(3)], axis=0
        )
        noisy = jnp.where(mcol > 0.5, masked, an[:HALF]).astype(BF16)

        for b in range(4):
            xo = 2 * h + b // 2
            zo = b % 2
            near = zo == p_x
            side = jnp.where(near, lax.rem(x + 1, 4), lax.rem(x + 3, 4))
            pos = jnp.where(
                xo == x,
                zo,
                jnp.where(xo == x2, 4 + zo, jnp.where(near, 0, 4) + jnp.where(xo == side, 2, 3)),
            )
            att[s, pos, pl.ds(0, 48), :] = clean[b * 48 : (b + 1) * 48]
            att[s, pos, pl.ds(48, 48), :] = noisy[b * 48 : (b + 1) * 48]

    own = None
    for n, k in enumerate((2, 1, 3, 0)):
        s = ys[k]
        finish(s, 0)
        finish(s, 1)
        for t in (1, 0):
            dst = abuf.at[:, :, pl.ds(pl.multiple_of((4 * t + y) * HEAD, HEAD), HEAD)]
            if (t, k) == (0, 0):
                own = pltpu.make_async_copy(att.at[s, pl.ds(0, 4)], dst, own_l)
                own.start()
            else:
                start(rcopy(att.at[s, pl.ds(4 * t, 4)], dst, a_s.at[4 * t + k], a_r.at[4 * t + y], adev[t][k]))
    own.wait()
    for t, k in ((0, 2), (1, 2), (0, 1), (1, 1), (0, 3), (1, 3), (1, 0)):
        slot = 4 * t + ys[k]
        dst = abuf.at[:, :, pl.ds(pl.multiple_of(slot * HEAD, HEAD), HEAD)]
        rcopy(att.at[0, pl.ds(0, 4)], dst, a_s.at[1], a_r.at[slot], cdev).wait_recv()

    def matmul(n):
        j, e = n // 2, n % 2
        if e == 0:
            wol[j].wait()
        cols = pl.ds(e * 512, 512)
        if j == 1:
            half = wp.at[1, :, cols]
            rcopy(half, half, wc_s.at[e], wc_r.at[e], cdev).wait_recv()
        if j == 2:
            half = wp.at[2, :, cols]
            rcopy(half, half, wy_s.at[e], wy_r.at[e], cdev).wait_recv()
            start(rcopy(half, wp.at[3, :, cols], wf_s.at[e], wf_r.at[e], cdev))
        if j == 3:
            half = wp.at[3, :, cols]
            rcopy(half, half, wf_s.at[e], wf_r.at[e], cdev).wait_recv()
        a = abuf[...].reshape(ROWS, 1024)
        r = jnp.dot(a[:, :512], wown[j, :, cols], preferred_element_type=F32)
        r = r + jnp.dot(a[:, 512:], wp[j, :, cols], preferred_element_type=F32)
        keep[n] = r[:192].reshape(2, 96, 512)
        xs[n, 0] = r[192:288].astype(BF16)
        xs[n, 1] = r[288:].astype(BF16)
        start(rcopy(xs.at[n, 0], xr.at[n, 0], x_s.at[n, 0], x_r.at[n, 0], xup))
        start(rcopy(xs.at[n, 1], xr.at[n, 1], x_s.at[n, 1], x_r.at[n, 1], xdn))

    from_below = lax.rem(x + 3, 4) // 2

    def reduce_x(n):
        for d in range(2):
            rcopy(xs.at[n, d], xr.at[n, d], x_s.at[n, d], x_r.at[n, d], xup).wait_recv()
        far = 1 - zh
        keep[n, zh] = keep[n, zh] + xr[n, (zh + from_below) % 2].astype(F32)
        zs[n] = (keep[n, far] + xr[n, (far + from_below) % 2].astype(F32)).astype(BF16)
        start(rcopy(zs.at[n], zr.at[n], z_s.at[n], z_r.at[n], hdev))

    def reduce_z(n):
        rcopy(zs.at[n], zr.at[n], z_s.at[n], z_r.at[n], hdev).wait_recv()
        total = (keep[n, zh] + zr[n].astype(F32)).astype(BF16)
        col = pl.multiple_of(order[n // 2] * 1024 + (n % 2) * 512, 512)
        out[:, pl.ds(col, 512)] = total[:48]
        out[:, pl.ds(4096 + col, 512)] = total[48:]

    for n in range(4):
        matmul(n)
    reduce_x(0)
    reduce_x(1)
    matmul(4)
    reduce_x(2)
    matmul(5)
    reduce_z(0)
    reduce_x(3)
    matmul(6)
    reduce_z(1)
    reduce_x(4)
    matmul(7)
    reduce_z(2)
    reduce_x(5)
    reduce_z(3)
    reduce_x(6)
    reduce_z(4)
    reduce_x(7)
    for n in (5, 6, 7):
        reduce_z(n)
    for cp in sends:
        cp.wait_send()


def vmem():
    return pl.BlockSpec(memory_space=pltpu.VMEM)


def anyspace():
    return pl.BlockSpec(memory_space=pl.ANY)


def shards(activations, noise_mask, span_order, mask_vector, input_weights, output_weight):
    dma = pltpu.SemaphoreType.DMA
    return pl.pallas_call(
        kernel,
        out_shape=jax.ShapeDtypeStruct((48, 8192), BF16),
        in_specs=[pl.BlockSpec(memory_space=pltpu.SMEM), anyspace(), vmem(), vmem(), anyspace(), anyspace()],
        out_specs=vmem(),
        scratch_shapes=[
            pltpu.VMEM((ROWS + 16, 4096), BF16),
            pltpu.VMEM((3, 4096, 512), BF16),
            pltpu.VMEM((3, 4, ROWS + 16, HEAD), BF16),
            pltpu.VMEM((16, 2, ROWS, HEAD), BF16),
            pltpu.VMEM((4, ROWS, HEAD), BF16),
            pltpu.VMEM((4, 8, ROWS), F32),
            pltpu.VMEM((8, QT, HEAD), BF16),
            pltpu.VMEM((8, QT, HEAD), F32),
            pltpu.VMEM((8, QT, 2 * HEAD), F32),
            pltpu.VMEM((4, 8, 96, HEAD), BF16),
            pltpu.VMEM((4, 96, 1024), BF16),
            pltpu.VMEM((4, 512, 1024), BF16),
            pltpu.VMEM((4, 512, 1024), BF16),
            pltpu.VMEM((8, 2, 96, 512), F32),
            pltpu.VMEM((8, 2, 96, 512), BF16),
            pltpu.VMEM((8, 2, 96, 512), BF16),
            pltpu.VMEM((8, 96, 512), BF16),
            pltpu.VMEM((8, 96, 512), BF16),
            dma((4,)),
            dma((6,)),
            dma((4,)),
            dma,
            dma((2, 4)),
            dma((2, 16)),
            dma((16,)),
            dma((4,)),
            dma((4,)),
            dma((4,)),
            dma((4,)),
            dma((2,)),
            dma((2,)),
            dma((8,)),
            dma((8,)),
            dma((8,)),
            dma((2,)),
            dma((2,)),
            dma((2,)),
            dma((2,)),
            dma((2,)),
            dma((2,)),
            dma((2,)),
            dma((2,)),
            dma((8, 2)),
            dma((8, 2)),
            dma((8,)),
            dma((8,)),
        ],
        compiler_params=pltpu.CompilerParams(
            collective_id=1, has_side_effects=True, vmem_limit_bytes=VMEM_BYTES
        ),
        name="whole",
    )(
        span_order,
        activations,
        noise_mask.reshape(1, ROWS),
        mask_vector.reshape(1, 4096),
        input_weights,
        output_weight,
    )


def solution(mesh):
    in_specs = (P("ctx", None), P("ctx"), P(), P(), P(None, None, "head"), P("head", None))
    out_specs = P(("ctx", "head"), None)
    return jax.shard_map(shards, mesh=mesh, in_specs=in_specs, out_specs=out_specs, check_vma=False)
```

```python
import functools
import math

import jax
import jax.numpy as jnp
from jax import lax
from jax.experimental import pallas as pl
from jax.experimental.pallas import tpu as pltpu
from jax.sharding import PartitionSpec as P

MESH = pl.DeviceIdType.MESH
HEAD = 128
ROWS = 384
HALF = 192
BLOCK = 64
QT = 208
NEG = -1e30
VMEM_BYTES = 60 << 20
NC = 256
LOG2_SCALE = math.log2(math.e) / math.sqrt(HEAD)
F32 = jnp.float32
BF16 = jnp.bfloat16


def coords():
    i = lax.axis_index("ctx")
    j = lax.axis_index("head")
    return j // 2, i // 4, (i // 2) % 2, j % 2, i % 2


def ctx_of(y, zl, c):
    return (y * 2 + zl) * 2 + c


def rcopy(src, dst, ssem, rsem, dev):
    return pltpu.make_async_remote_copy(
        src_ref=src, dst_ref=dst, send_sem=ssem, recv_sem=rsem, device_id=dev, device_id_type=MESH
    )


def greet(devs):
    barrier = pltpu.get_barrier_semaphore()
    for dev in devs:
        pl.semaphore_signal(barrier, inc=1, device_id=dev, device_id_type=MESH)
    return lambda: pl.semaphore_wait(barrier, len(devs))


def kernel(
    span, act, nmask, mvec, w, wo, out,
    lhs, wbuf, st, kv, q, msk, qt, m_ref, o_ref, att, abuf, wown, wp, keep, xs, xr, zs, zr,
    act_l, w_l, wo_l, own_l, f_s, f_r, g_r, q_s, q_r, m_s, m_r, zk_s, zf_s, c_s, a_s, a_r,
    wx_s, wx_r, wc_s, wc_r, wy_s, wy_r, wf_s, wf_r, x_s, x_r, z_s, z_r,
):
    x, y, zl, zh, c = coords()
    hd = lax.axis_index("head")
    me = ctx_of(y, zl, c)
    ys = [y] + [lax.rem(y + k, 4) for k in (1, 2, 3)]
    x2 = lax.rem(x + 2, 4)
    ydev = [(ctx_of(ys[k], zl, c), hd) for k in range(4)]
    adev = [ydev, [(ctx_of(ys[k], zl, c), x2 * 2 + zh) for k in range(4)]]
    zdev = (ctx_of(y, 1 - zl, c), hd)
    ddev = (ctx_of(ys[2], 1 - zl, c), hd)
    cdev = (ctx_of(y, zl, 1 - c), hd)
    xup = (me, lax.rem(x + 1, 4) * 2 + zh)
    xdn = (me, lax.rem(x + 3, 4) * 2 + zh)
    hdev = (me, x * 2 + 1 - zh)
    wydev = (ctx_of(lax.rem(y + 1 + 2 * c, 4), zl, c), hd)
    arrive = greet(ydev[1:] + adev[1] + [zdev, ddev, cdev, xup, xdn, hdev])

    sends = []

    def start(cp):
        cp.start()
        sends.append(cp)

    loads = []
    for kc in range(4):
        part = pl.ds(kc * 1024, 1024)
        loads.append(
            (
                pltpu.make_async_copy(act.at[:, part], lhs.at[pl.ds(0, ROWS), part], act_l.at[kc]),
                pltpu.make_async_copy(w.at[0, part], wbuf.at[0, part], w_l.at[kc]),
            )
        )
    wk = pltpu.make_async_copy(w.at[1], wbuf.at[1], w_l.at[4])
    wv = pltpu.make_async_copy(w.at[2], wbuf.at[2], w_l.at[5])
    qd = lax.rem(y, 2) * 2 + c
    order = (qd, qd + 1 - 2 * c, lax.rem(qd + 2, 4), lax.rem(qd + 2, 4) + 1 - 2 * c)
    wol = []
    for n in range(4):
        col = pl.multiple_of(order[n] * 1024, 1024)
        wol.append(pltpu.make_async_copy(wo.at[:, pl.ds(col, 1024)], wown.at[n], wo_l.at[n]))

    def load(*copies):
        for cp in copies:
            cp.start()

    load(*loads[0], *loads[1], *loads[2])
    lhs[pl.ds(ROWS, 16), :] = jnp.broadcast_to(mvec[...].reshape(1, 4096), (16, 4096))
    msk[y] = jnp.broadcast_to(nmask[...].astype(F32).reshape(1, ROWS), (8, ROWS))

    def keep_heads(m, r):
        for j in range(4):
            st[m, j] = r[:, j * HEAD : (j + 1) * HEAD].astype(BF16)

    arrive()
    for e in range(2):
        col = pl.multiple_of(qd * 1024 + e * 512, 512)
        half = wp.at[0, :, pl.ds(e * 512, 512)]
        start(rcopy(wo.at[:, pl.ds(col, 512)], half, wx_s.at[e], wx_r.at[e], adev[1][0]))

    rows = pl.ds(0, ROWS)
    r = None
    for kc in range(4):
        for cp in loads[kc]:
            cp.wait()
        if kc == 0:
            load(*loads[3])
        if kc == 1:
            load(wk)
        part = pl.ds(kc * 1024, 1024)
        d = jnp.dot(lhs[:, part], wbuf[0, part], preferred_element_type=F32)
        r = d if r is None else r + d
    load(wv)
    keep_heads(0, r * LOG2_SCALE)
    for k in (1, 3, 2):
        start(rcopy(st.at[0, ys[k], rows], q.at[y], q_s.at[k], q_r.at[y], ydev[k]))
        start(rcopy(msk.at[y], msk.at[y], m_s.at[k], m_r.at[y], ydev[k]))
    q[y] = st[0, y, rows]

    for m, cp in ((1, wk), (2, wv)):
        cp.wait()
        if m == 2:
            load(*wol)
        keep_heads(m, jnp.dot(lhs[...], wbuf[m], preferred_element_type=F32))
        dst = kv.at[me, m - 1]
        start(rcopy(st.at[m, y, rows], dst, zk_s.at[m - 1], f_r.at[m - 1, me], zdev))
        for k in (1, 3):
            start(rcopy(st.at[m, ys[k], rows], dst, f_s.at[m - 1, k], f_r.at[m - 1, me], ydev[k]))
        kv[me, m - 1] = st[m, y, rows]
    start(rcopy(kv.at[me], kv.at[me], c_s.at[0], g_r.at[me], cdev))
    for m in (1, 2):
        dst = kv.at[me, m - 1]
        start(rcopy(st.at[m, ys[2], rows], dst, f_s.at[m - 1, 2], f_r.at[m - 1, me], ydev[2]))
        start(rcopy(st.at[m, ys[2], rows], dst, f_s.at[m - 1, 0], f_r.at[m - 1, me], ddev))
    def here(k, z, split):
        slot = ctx_of(ys[k], z, c)
        if split:
            for m in range(2):
                rcopy(kv.at[slot, m], kv.at[slot, m], zk_s.at[m], f_r.at[m, slot], cdev).wait_recv()
        else:
            rcopy(kv.at[slot], kv.at[slot], zk_s.at[0], g_r.at[slot], cdev).wait_recv()
        return slot

    def to_core(n, slot):
        start(rcopy(kv.at[slot], kv.at[slot], c_s.at[n], g_r.at[slot], cdev))

    def to_z(n, slot):
        start(rcopy(kv.at[slot], kv.at[slot], zf_s.at[n], g_r.at[slot], zdev))

    def from_core(k, z):
        slot = ctx_of(ys[k], z, 1 - c)
        rcopy(kv.at[slot], kv.at[slot], zk_s.at[0], g_r.at[slot], cdev).wait_recv()

    def send_wp(e):
        half = wp.at[0, :, pl.ds(e * 512, 512)]
        rcopy(half, half, wx_s.at[e], wx_r.at[e], cdev).wait_recv()
        start(rcopy(half, wp.at[1, :, pl.ds(e * 512, 512)], wc_s.at[e], wc_r.at[e], cdev))
        start(rcopy(half, wp.at[2, :, pl.ds(e * 512, 512)], wy_s.at[e], wy_r.at[e], wydev))

    def chunk(pa, pb):
        place = lax.broadcasted_iota(jnp.int32, (1, 4 * ROWS), 1) // HALF
        ks = jnp.zeros((1, 4 * ROWS), jnp.int32)
        for n in range(8):
            ks = jnp.where(place == n, span[4 * (pa if n < 4 else pb) + n % 4], ks)
        refs = [(p, m) for m in range(2) for p in (pa, pb)]
        got = [kv[pl.ds(2 * p, 2), m].reshape(2 * ROWS, HEAD) for p, m in refs]
        k = jnp.concatenate(got[:2], axis=0)
        v = jnp.concatenate(got[2:], axis=0)
        return k, jnp.concatenate([v, jnp.ones((4 * ROWS, HEAD), BF16)], axis=1), ks

    def attend(i, u, keys, first):
        k, v, ks = keys
        sc = lax.dot_general(qt[i], k, (((1,), (1,)), ((), ())), preferred_element_type=F32)
        sc = sc + jnp.where(ks < u, F32(0), F32(NEG))
        top = jnp.max(sc, axis=1, keepdims=True)
        if first:
            new = jnp.maximum(top, F32(NEG))
        else:
            old = m_ref[i][:, :1]
            new = jnp.maximum(old, top)
        p = jnp.exp2(sc - new).astype(BF16)
        o = jnp.dot(p, v, preferred_element_type=F32)
        if not first:
            o = o_ref[i] * jnp.exp2(old - new) + o
        return new, o

    def step(pa, pb, first):
        keys = chunk(pa, pb)
        for i in range(8):
            u = span[2 * ctx_of(i // 2, zl, c) + i % 2]
            new, o = attend(i, u, keys, first)
            m_ref[i] = jnp.broadcast_to(new, (QT, HEAD))
            o_ref[i] = o

    def pair(k, z):
        return ys[k] * 2 + z

    to_core(1, here(0, 1 - zl, True))
    for n, k in ((0, 1), (1, 3)):
        slot = here(k, zl, True)
        to_z(n, slot)
        to_core(2 + n, slot)
    for k in (1, 3, 2):
        rcopy(q.at[ys[k]], q.at[ys[k]], q_s.at[1], q_r.at[ys[k]], cdev).wait_recv()
        rcopy(msk.at[ys[k]], msk.at[ys[k]], m_s.at[1], m_r.at[ys[k]], cdev).wait_recv()
    for s in range(4):
        for h in range(2):
            qt[2 * s + h, pl.ds(0, HALF), :] = q[s, pl.ds(h * HALF, HALF), :]
            qt[2 * s + h, pl.ds(HALF, 16), :] = st[0, y, pl.ds(ROWS, 16), :]
    from_core(0, zl)
    from_core(0, 1 - zl)
    step(pair(0, zl), pair(0, 1 - zl), True)
    send_wp(0)
    from_core(1, zl)
    from_core(3, zl)
    step(pair(1, zl), pair(3, zl), False)
    to_core(4, here(2, zl, True))
    to_core(5, here(1, 1 - zl, False))
    from_core(2, zl)
    from_core(1, 1 - zl)
    step(pair(2, zl), pair(1, 1 - zl), False)
    to_core(6, here(3, 1 - zl, False))
    to_core(7, here(2, 1 - zl, True))
    send_wp(1)
    from_core(3, 1 - zl)
    from_core(2, 1 - zl)

    p_x = x // 2
    km = st[1, y, pl.ds(ROWS, 16), :]
    vm = st[2, y, pl.ds(ROWS, 16), :][:1].astype(F32)
    vm = jnp.concatenate([vm, jnp.ones((1, HEAD), F32)], axis=1)
    rowi = lax.broadcasted_iota(jnp.int32, (QT, HALF), 0)
    coli = lax.broadcasted_iota(jnp.int32, (QT, HALF), 1)
    bi = jnp.where(rowi < HALF, rowi // BLOCK, jnp.minimum(rowi - HALF, 2))
    bj = coli // BLOCK
    last = chunk(pair(3, 1 - zl), pair(2, 1 - zl))

    def finish(s, h):
        i = 2 * s + h
        src = ctx_of(s, zl, c)
        mp, op = attend(i, span[2 * src + h], last, False)
        qi = qt[i]
        ko = kv[src, 0, pl.ds(h * HALF, HALF), :]
        vo = jnp.concatenate([kv[src, 1, pl.ds(h * HALF, HALF), :], jnp.ones((HALF, HEAD), BF16)], axis=1)
        so = lax.dot_general(qi, ko, (((1,), (1,)), ((), ())), preferred_element_type=F32)
        sm = lax.dot_general(qi, km, (((1,), (1,)), ((), ())), preferred_element_type=F32)[:, :1]
        mrow = msk[s, pl.ds(0, 1), pl.ds(h * HALF, HALF)]

        sc = jnp.where(bj <= bi, so, F32(NEG))
        mc = jnp.maximum(mp, jnp.max(sc, axis=1, keepdims=True))
        pc = jnp.where(bj <= bi, jnp.exp2(sc - mc), F32(0)).astype(BF16)
        oc = op * jnp.exp2(mp - mc) + jnp.dot(pc, vo, preferred_element_type=F32)
        clean = (oc[:HALF, :HEAD] / oc[:HALF, HEAD:]).astype(BF16)

        hit = (bj == bi) & (mrow > 0.5)
        sn = jnp.where(hit, sm, sc)
        mn = jnp.maximum(mp, jnp.max(sn, axis=1, keepdims=True))
        pn = jnp.where(bj <= bi, jnp.exp2(sn - mn), F32(0)).astype(BF16)
        pz = jnp.where(hit, F32(0), pn.astype(F32))
        wm = jnp.sum(pn.astype(F32) - pz, axis=1, keepdims=True)
        on = op * jnp.exp2(mp - mn) + jnp.dot(pz.astype(BF16), vo, preferred_element_type=F32) + wm * vm
        an = on[:, :HEAD] / on[:, HEAD:]
        mcol = jnp.sum(jnp.where(rowi == coli, mrow, F32(0)), axis=1, keepdims=True)[:HALF]
        masked = jnp.concatenate(
            [jnp.broadcast_to(an[HALF + b : HALF + b + 1], (BLOCK, HEAD)) for b in range(3)], axis=0
        )
        noisy = jnp.where(mcol > 0.5, masked, an[:HALF]).astype(BF16)

        for b in range(4):
            xo = 2 * h + b // 2
            zo = b % 2
            near = zo == p_x
            side = jnp.where(near, lax.rem(x + 1, 4), lax.rem(x + 3, 4))
            pos = jnp.where(
                xo == x,
                zo,
                jnp.where(xo == x2, 4 + zo, jnp.where(near, 0, 4) + jnp.where(xo == side, 2, 3)),
            )
            att[s, pos, pl.ds(0, 48), :] = clean[b * 48 : (b + 1) * 48]
            att[s, pos, pl.ds(48, 48), :] = noisy[b * 48 : (b + 1) * 48]

    own = None
    for n, k in enumerate((2, 1, 3, 0)):
        s = ys[k]
        finish(s, 0)
        finish(s, 1)
        for t in (1, 0):
            dst = abuf.at[:, :, pl.ds(pl.multiple_of((4 * t + y) * HEAD, HEAD), HEAD)]
            if (t, k) == (0, 0):
                own = pltpu.make_async_copy(att.at[s, pl.ds(0, 4)], dst, own_l)
                own.start()
            else:
                start(rcopy(att.at[s, pl.ds(4 * t, 4)], dst, a_s.at[4 * t + k], a_r.at[4 * t + y], adev[t][k]))
    own.wait()
    for t, k in ((0, 2), (1, 2), (0, 1), (1, 1), (0, 3), (1, 3), (1, 0)):
        slot = 4 * t + ys[k]
        dst = abuf.at[:, :, pl.ds(pl.multiple_of(slot * HEAD, HEAD), HEAD)]
        rcopy(att.at[0, pl.ds(0, 4)], dst, a_s.at[1], a_r.at[slot], cdev).wait_recv()

    def matmul(n):
        j, e = n // 4, n // 2 % 2
        if n % 4 == 0:
            wol[j].wait()
        half = wp.at[j, :, pl.ds(e * 512, 512)]
        if n % 2 == 0 and j == 1:
            rcopy(half, half, wc_s.at[e], wc_r.at[e], cdev).wait_recv()
        if n % 2 == 0 and j == 2:
            rcopy(half, half, wy_s.at[e], wy_r.at[e], cdev).wait_recv()
            start(rcopy(half, wp.at[3, :, pl.ds(e * 512, 512)], wf_s.at[e], wf_r.at[e], cdev))
        if n % 2 == 0 and j == 3:
            rcopy(half, half, wf_s.at[e], wf_r.at[e], cdev).wait_recv()
        cols = pl.ds(n % 4 * NC, NC)
        a = abuf[...].reshape(ROWS, 1024)
        r = jnp.dot(a[:, :512], wown[j, :, cols], preferred_element_type=F32)
        r = r + jnp.dot(a[:, 512:], wp[j, :, cols], preferred_element_type=F32)
        keep[n] = r[:192].reshape(2, 96, NC)
        xs[n, 0] = r[192:288].astype(BF16)
        xs[n, 1] = r[288:].astype(BF16)
        start(rcopy(xs.at[n, 0], xr.at[n, 0], x_s.at[n, 0], x_r.at[n, 0], xup))
        start(rcopy(xs.at[n, 1], xr.at[n, 1], x_s.at[n, 1], x_r.at[n, 1], xdn))

    from_below = lax.rem(x + 3, 4) // 2

    def reduce_x(n):
        for d in range(2):
            rcopy(xs.at[n, d], xr.at[n, d], x_s.at[n, d], x_r.at[n, d], xup).wait_recv()
        far = 1 - zh
        keep[n, zh] = keep[n, zh] + xr[n, (zh + from_below) % 2].astype(F32)
        zs[n] = (keep[n, far] + xr[n, (far + from_below) % 2].astype(F32)).astype(BF16)
        start(rcopy(zs.at[n], zr.at[n], z_s.at[n], z_r.at[n], hdev))

    def reduce_z(n):
        rcopy(zs.at[n], zr.at[n], z_s.at[n], z_r.at[n], hdev).wait_recv()
        total = (keep[n, zh] + zr[n].astype(F32)).astype(BF16)
        col = pl.multiple_of(order[n // 4] * 1024 + n % 4 * NC, NC)
        out[:, pl.ds(col, NC)] = total[:48]
        out[:, pl.ds(4096 + col, NC)] = total[48:]

    for n in range(4):
        matmul(n)
    for n in range(16):
        reduce_x(n)
        if n + 4 < 16:
            matmul(n + 4)
        if n >= 3:
            reduce_z(n - 3)
    for n in (13, 14, 15):
        reduce_z(n)
    for cp in sends:
        cp.wait_send()


def vmem():
    return pl.BlockSpec(memory_space=pltpu.VMEM)


def anyspace():
    return pl.BlockSpec(memory_space=pl.ANY)


def shards(activations, noise_mask, span_order, mask_vector, input_weights, output_weight):
    dma = pltpu.SemaphoreType.DMA
    return pl.pallas_call(
        kernel,
        out_shape=jax.ShapeDtypeStruct((48, 8192), BF16),
        in_specs=[pl.BlockSpec(memory_space=pltpu.SMEM), anyspace(), vmem(), vmem(), anyspace(), anyspace()],
        out_specs=vmem(),
        scratch_shapes=[
            pltpu.VMEM((ROWS + 16, 4096), BF16),
            pltpu.VMEM((3, 4096, 512), BF16),
            pltpu.VMEM((3, 4, ROWS + 16, HEAD), BF16),
            pltpu.VMEM((16, 2, ROWS, HEAD), BF16),
            pltpu.VMEM((4, ROWS, HEAD), BF16),
            pltpu.VMEM((4, 8, ROWS), F32),
            pltpu.VMEM((8, QT, HEAD), BF16),
            pltpu.VMEM((8, QT, HEAD), F32),
            pltpu.VMEM((8, QT, 2 * HEAD), F32),
            pltpu.VMEM((4, 8, 96, HEAD), BF16),
            pltpu.VMEM((4, 96, 1024), BF16),
            pltpu.VMEM((4, 512, 1024), BF16),
            pltpu.VMEM((4, 512, 1024), BF16),
            pltpu.VMEM((16, 2, 96, NC), F32),
            pltpu.VMEM((16, 2, 96, NC), BF16),
            pltpu.VMEM((16, 2, 96, NC), BF16),
            pltpu.VMEM((16, 96, NC), BF16),
            pltpu.VMEM((16, 96, NC), BF16),
            dma((4,)),
            dma((6,)),
            dma((4,)),
            dma,
            dma((2, 4)),
            dma((2, 16)),
            dma((16,)),
            dma((4,)),
            dma((4,)),
            dma((4,)),
            dma((4,)),
            dma((2,)),
            dma((2,)),
            dma((8,)),
            dma((8,)),
            dma((8,)),
            dma((2,)),
            dma((2,)),
            dma((2,)),
            dma((2,)),
            dma((2,)),
            dma((2,)),
            dma((2,)),
            dma((2,)),
            dma((16, 2)),
            dma((16, 2)),
            dma((16,)),
            dma((16,)),
        ],
        compiler_params=pltpu.CompilerParams(
            collective_id=1, has_side_effects=True, vmem_limit_bytes=VMEM_BYTES
        ),
        name="whole",
    )(
        span_order,
        activations,
        noise_mask,
        mask_vector,
        input_weights,
        output_weight,
    )


def solution(mesh):
    in_specs = (P("ctx", None), P("ctx"), P(), P(), P(None, None, "head"), P("head", None))
    out_specs = P(("ctx", "head"), None)
    return jax.shard_map(shards, mesh=mesh, in_specs=in_specs, out_specs=out_specs, check_vma=False)
```

```python
import functools
import math

import jax
import jax.numpy as jnp
from jax import lax
from jax.experimental import pallas as pl
from jax.experimental.pallas import tpu as pltpu
from jax.sharding import PartitionSpec as P

MESH = pl.DeviceIdType.MESH
HEAD = 128
ROWS = 384
HALF = 192
BLOCK = 64
QT = 208
NEG = -1e30
VMEM_BYTES = 60 << 20
NC = 256
LOG2_SCALE = math.log2(math.e) / math.sqrt(HEAD)
F32 = jnp.float32
BF16 = jnp.bfloat16


def coords():
    i = lax.axis_index("ctx")
    j = lax.axis_index("head")
    return j // 2, i // 4, (i // 2) % 2, j % 2, i % 2


def ctx_of(y, zl, c):
    return (y * 2 + zl) * 2 + c


def rcopy(src, dst, ssem, rsem, dev):
    return pltpu.make_async_remote_copy(
        src_ref=src, dst_ref=dst, send_sem=ssem, recv_sem=rsem, device_id=dev, device_id_type=MESH
    )


def greet(devs):
    barrier = pltpu.get_barrier_semaphore()
    for dev in devs:
        pl.semaphore_signal(barrier, inc=1, device_id=dev, device_id_type=MESH)
    return lambda: pl.semaphore_wait(barrier, len(devs))


def kernel(
    span, act, nmask, mvec, w, wo, out,
    lhs, wbuf, st, kv, q, msk, qt, m_ref, o_ref, att, abuf, wown, wp, keep, xs, xr, zs, zr,
    act_l, w_l, wo_l, own_l, f_s, f_r, g_r, q_s, q_r, m_s, m_r, zk_s, zf_s, c_s, a_s, a_r,
    wx_s, wx_r, wc_s, wc_r, wy_s, wy_r, wf_s, wf_r, x_s, x_r, z_s, z_r,
):
    x, y, zl, zh, c = coords()
    hd = lax.axis_index("head")
    me = ctx_of(y, zl, c)
    ys = [y] + [lax.rem(y + k, 4) for k in (1, 2, 3)]
    x2 = lax.rem(x + 2, 4)
    ydev = [(ctx_of(ys[k], zl, c), hd) for k in range(4)]
    adev = [ydev, [(ctx_of(ys[k], zl, c), x2 * 2 + zh) for k in range(4)]]
    zdev = (ctx_of(y, 1 - zl, c), hd)
    ddev = (ctx_of(ys[2], 1 - zl, c), hd)
    cdev = (ctx_of(y, zl, 1 - c), hd)
    xup = (me, lax.rem(x + 1, 4) * 2 + zh)
    xdn = (me, lax.rem(x + 3, 4) * 2 + zh)
    hdev = (me, x * 2 + 1 - zh)
    wydev = (ctx_of(lax.rem(y + 1 + 2 * c, 4), zl, c), hd)
    arrive = greet(ydev[1:] + adev[1] + [zdev, ddev, cdev, xup, xdn, hdev])

    sends = []

    def start(cp):
        cp.start()
        sends.append(cp)

    loads = []
    for kc in range(4):
        part = pl.ds(kc * 1024, 1024)
        loads.append(
            (
                pltpu.make_async_copy(act.at[:, part], lhs.at[pl.ds(0, ROWS), part], act_l.at[kc]),
                pltpu.make_async_copy(w.at[0, part], wbuf.at[0, part], w_l.at[kc]),
            )
        )
    wk = pltpu.make_async_copy(w.at[1], wbuf.at[1], w_l.at[4])
    wv = pltpu.make_async_copy(w.at[2], wbuf.at[2], w_l.at[5])
    qd = lax.rem(y, 2) * 2 + c
    order = (qd, qd + 1 - 2 * c, lax.rem(qd + 2, 4), lax.rem(qd + 2, 4) + 1 - 2 * c)
    wol = []
    for n in range(4):
        col = pl.multiple_of(order[n] * 1024, 1024)
        wol.append(pltpu.make_async_copy(wo.at[:, pl.ds(col, 1024)], wown.at[n], wo_l.at[n]))

    def load(*copies):
        for cp in copies:
            cp.start()

    load(*loads[0], *loads[1], *loads[2])
    lhs[pl.ds(ROWS, 16), :] = jnp.broadcast_to(mvec[...].reshape(1, 4096), (16, 4096))
    msk[y] = jnp.broadcast_to(nmask[...].astype(F32).reshape(1, ROWS), (8, ROWS))

    def keep_heads(m, r):
        for j in range(4):
            st[m, j] = r[:, j * HEAD : (j + 1) * HEAD].astype(BF16)

    arrive()
    for e in range(2):
        col = pl.multiple_of(qd * 1024 + e * 512, 512)
        half = wp.at[0, :, pl.ds(e * 512, 512)]
        start(rcopy(wo.at[:, pl.ds(col, 512)], half, wx_s.at[e], wx_r.at[e], adev[1][0]))

    rows = pl.ds(0, ROWS)
    r = None
    for kc in range(4):
        for cp in loads[kc]:
            cp.wait()
        if kc == 0:
            load(*loads[3])
        if kc == 1:
            load(wk)
        part = pl.ds(kc * 1024, 1024)
        d = jnp.dot(lhs[:, part], wbuf[0, part], preferred_element_type=F32)
        r = d if r is None else r + d
    load(wv)
    keep_heads(0, r * LOG2_SCALE)
    for k in (1, 3, 2):
        start(rcopy(st.at[0, ys[k], rows], q.at[y], q_s.at[k], q_r.at[y], ydev[k]))
        start(rcopy(msk.at[y], msk.at[y], m_s.at[k], m_r.at[y], ydev[k]))
    q[y] = st[0, y, rows]

    for m, cp in ((1, wk), (2, wv)):
        cp.wait()
        if m == 2:
            load(*wol)
        keep_heads(m, jnp.dot(lhs[...], wbuf[m], preferred_element_type=F32))
        dst = kv.at[me, m - 1]
        start(rcopy(st.at[m, y, rows], dst, zk_s.at[m - 1], f_r.at[m - 1, me], zdev))
        for k in (1, 3):
            start(rcopy(st.at[m, ys[k], rows], dst, f_s.at[m - 1, k], f_r.at[m - 1, me], ydev[k]))
        kv[me, m - 1] = st[m, y, rows]
    start(rcopy(kv.at[me], kv.at[me], c_s.at[0], g_r.at[me], cdev))
    def here(k, z, split):
        slot = ctx_of(ys[k], z, c)
        if split:
            for m in range(2):
                rcopy(kv.at[slot, m], kv.at[slot, m], zk_s.at[m], f_r.at[m, slot], cdev).wait_recv()
        else:
            rcopy(kv.at[slot], kv.at[slot], zk_s.at[0], g_r.at[slot], cdev).wait_recv()
        return slot

    def to_core(n, slot):
        start(rcopy(kv.at[slot], kv.at[slot], c_s.at[n], g_r.at[slot], cdev))

    def to_z(n, slot):
        start(rcopy(kv.at[slot], kv.at[slot], zf_s.at[n], g_r.at[slot], zdev))

    def from_core(k, z):
        slot = ctx_of(ys[k], z, 1 - c)
        rcopy(kv.at[slot], kv.at[slot], zk_s.at[0], g_r.at[slot], cdev).wait_recv()

    def send_wp(e):
        half = wp.at[0, :, pl.ds(e * 512, 512)]
        rcopy(half, half, wx_s.at[e], wx_r.at[e], cdev).wait_recv()
        start(rcopy(half, wp.at[1, :, pl.ds(e * 512, 512)], wc_s.at[e], wc_r.at[e], cdev))
        start(rcopy(half, wp.at[2, :, pl.ds(e * 512, 512)], wy_s.at[e], wy_r.at[e], wydev))

    def chunk(pa, pb):
        place = lax.broadcasted_iota(jnp.int32, (1, 4 * ROWS), 1) // HALF
        ks = jnp.zeros((1, 4 * ROWS), jnp.int32)
        for n in range(8):
            ks = jnp.where(place == n, span[4 * (pa if n < 4 else pb) + n % 4], ks)
        refs = [(p, m) for m in range(2) for p in (pa, pb)]
        got = [kv[pl.ds(2 * p, 2), m].reshape(2 * ROWS, HEAD) for p, m in refs]
        k = jnp.concatenate(got[:2], axis=0)
        v = jnp.concatenate(got[2:], axis=0)
        return k, jnp.concatenate([v, jnp.ones((4 * ROWS, HEAD), BF16)], axis=1), ks

    def attend(i, u, keys, first):
        k, v, ks = keys
        sc = lax.dot_general(qt[i], k, (((1,), (1,)), ((), ())), preferred_element_type=F32)
        sc = sc + jnp.where(ks < u, F32(0), F32(NEG))
        top = jnp.max(sc, axis=1, keepdims=True)
        if first:
            new = jnp.maximum(top, F32(NEG))
        else:
            old = m_ref[i][:, :1]
            new = jnp.maximum(old, top)
        p = jnp.exp2(sc - new).astype(BF16)
        o = jnp.dot(p, v, preferred_element_type=F32)
        if not first:
            o = o_ref[i] * jnp.exp2(old - new) + o
        return new, o

    def step(pa, pb, first):
        keys = chunk(pa, pb)
        for i in range(8):
            u = span[2 * ctx_of(i // 2, zl, c) + i % 2]
            new, o = attend(i, u, keys, first)
            m_ref[i] = jnp.broadcast_to(new, (QT, HEAD))
            o_ref[i] = o

    def pair(k, z):
        return ys[k] * 2 + z

    to_core(1, here(0, 1 - zl, True))
    for n, k in ((0, 1), (1, 3)):
        slot = here(k, zl, True)
        to_z(n, slot)
        to_core(2 + n, slot)
    for m in (1, 2):
        dst = kv.at[me, m - 1]
        start(rcopy(st.at[m, ys[2], rows], dst, f_s.at[m - 1, 2], f_r.at[m - 1, me], ydev[2]))
        start(rcopy(st.at[m, ys[2], rows], dst, f_s.at[m - 1, 0], f_r.at[m - 1, me], ddev))
    for k in (1, 3, 2):
        rcopy(q.at[ys[k]], q.at[ys[k]], q_s.at[1], q_r.at[ys[k]], cdev).wait_recv()
        rcopy(msk.at[ys[k]], msk.at[ys[k]], m_s.at[1], m_r.at[ys[k]], cdev).wait_recv()
    for s in range(4):
        for h in range(2):
            qt[2 * s + h, pl.ds(0, HALF), :] = q[s, pl.ds(h * HALF, HALF), :]
            qt[2 * s + h, pl.ds(HALF, 16), :] = st[0, y, pl.ds(ROWS, 16), :]
    from_core(0, zl)
    from_core(0, 1 - zl)
    step(pair(0, zl), pair(0, 1 - zl), True)
    from_core(1, zl)
    from_core(3, zl)
    step(pair(1, zl), pair(3, zl), False)
    to_core(4, here(2, zl, True))
    to_core(5, here(1, 1 - zl, False))
    send_wp(0)
    from_core(2, zl)
    from_core(1, 1 - zl)
    step(pair(2, zl), pair(1, 1 - zl), False)
    to_core(6, here(3, 1 - zl, False))
    to_core(7, here(2, 1 - zl, True))
    send_wp(1)
    from_core(3, 1 - zl)
    from_core(2, 1 - zl)

    p_x = x // 2
    km = st[1, y, pl.ds(ROWS, 16), :]
    vm = st[2, y, pl.ds(ROWS, 16), :][:1].astype(F32)
    vm = jnp.concatenate([vm, jnp.ones((1, HEAD), F32)], axis=1)
    rowi = lax.broadcasted_iota(jnp.int32, (QT, HALF), 0)
    coli = lax.broadcasted_iota(jnp.int32, (QT, HALF), 1)
    bi = jnp.where(rowi < HALF, rowi // BLOCK, jnp.minimum(rowi - HALF, 2))
    bj = coli // BLOCK
    last = chunk(pair(3, 1 - zl), pair(2, 1 - zl))

    def finish(s, h):
        i = 2 * s + h
        src = ctx_of(s, zl, c)
        mp, op = attend(i, span[2 * src + h], last, False)
        qi = qt[i]
        ko = kv[src, 0, pl.ds(h * HALF, HALF), :]
        vo = jnp.concatenate([kv[src, 1, pl.ds(h * HALF, HALF), :], jnp.ones((HALF, HEAD), BF16)], axis=1)
        so = lax.dot_general(qi, ko, (((1,), (1,)), ((), ())), preferred_element_type=F32)
        sm = lax.dot_general(qi, km, (((1,), (1,)), ((), ())), preferred_element_type=F32)[:, :1]
        mrow = msk[s, pl.ds(0, 1), pl.ds(h * HALF, HALF)]

        sc = jnp.where(bj <= bi, so, F32(NEG))
        mc = jnp.maximum(mp, jnp.max(sc, axis=1, keepdims=True))
        pc = jnp.where(bj <= bi, jnp.exp2(sc - mc), F32(0)).astype(BF16)
        oc = op * jnp.exp2(mp - mc) + jnp.dot(pc, vo, preferred_element_type=F32)
        clean = (oc[:HALF, :HEAD] / oc[:HALF, HEAD:]).astype(BF16)

        hit = (bj == bi) & (mrow > 0.5)
        sn = jnp.where(hit, sm, sc)
        mn = jnp.maximum(mp, jnp.max(sn, axis=1, keepdims=True))
        pn = jnp.where(bj <= bi, jnp.exp2(sn - mn), F32(0)).astype(BF16)
        pz = jnp.where(hit, F32(0), pn.astype(F32))
        wm = jnp.sum(pn.astype(F32) - pz, axis=1, keepdims=True)
        on = op * jnp.exp2(mp - mn) + jnp.dot(pz.astype(BF16), vo, preferred_element_type=F32) + wm * vm
        an = on[:, :HEAD] / on[:, HEAD:]
        mcol = jnp.sum(jnp.where(rowi == coli, mrow, F32(0)), axis=1, keepdims=True)[:HALF]
        masked = jnp.concatenate(
            [jnp.broadcast_to(an[HALF + b : HALF + b + 1], (BLOCK, HEAD)) for b in range(3)], axis=0
        )
        noisy = jnp.where(mcol > 0.5, masked, an[:HALF]).astype(BF16)

        for b in range(4):
            xo = 2 * h + b // 2
            zo = b % 2
            near = zo == p_x
            side = jnp.where(near, lax.rem(x + 1, 4), lax.rem(x + 3, 4))
            pos = jnp.where(
                xo == x,
                zo,
                jnp.where(xo == x2, 4 + zo, jnp.where(near, 0, 4) + jnp.where(xo == side, 2, 3)),
            )
            att[s, pos, pl.ds(0, 48), :] = clean[b * 48 : (b + 1) * 48]
            att[s, pos, pl.ds(48, 48), :] = noisy[b * 48 : (b + 1) * 48]

    own = None
    for n, k in enumerate((2, 1, 3, 0)):
        s = ys[k]
        finish(s, 0)
        finish(s, 1)
        for t in (1, 0):
            dst = abuf.at[:, :, pl.ds(pl.multiple_of((4 * t + y) * HEAD, HEAD), HEAD)]
            if (t, k) == (0, 0):
                own = pltpu.make_async_copy(att.at[s, pl.ds(0, 4)], dst, own_l)
                own.start()
            else:
                start(rcopy(att.at[s, pl.ds(4 * t, 4)], dst, a_s.at[4 * t + k], a_r.at[4 * t + y], adev[t][k]))
    own.wait()
    for t, k in ((0, 2), (1, 2), (0, 1), (1, 1), (0, 3), (1, 3), (1, 0)):
        slot = 4 * t + ys[k]
        dst = abuf.at[:, :, pl.ds(pl.multiple_of(slot * HEAD, HEAD), HEAD)]
        rcopy(att.at[0, pl.ds(0, 4)], dst, a_s.at[1], a_r.at[slot], cdev).wait_recv()

    def matmul(n):
        j, e = n // 4, n // 2 % 2
        if n % 4 == 0:
            wol[j].wait()
        half = wp.at[j, :, pl.ds(e * 512, 512)]
        if n % 2 == 0 and j == 1:
            rcopy(half, half, wc_s.at[e], wc_r.at[e], cdev).wait_recv()
        if n % 2 == 0 and j == 2:
            rcopy(half, half, wy_s.at[e], wy_r.at[e], cdev).wait_recv()
            start(rcopy(half, wp.at[3, :, pl.ds(e * 512, 512)], wf_s.at[e], wf_r.at[e], cdev))
        if n % 2 == 0 and j == 3:
            rcopy(half, half, wf_s.at[e], wf_r.at[e], cdev).wait_recv()
        cols = pl.ds(n % 4 * NC, NC)
        a = abuf[...].reshape(ROWS, 1024)
        r = jnp.dot(a[:, :512], wown[j, :, cols], preferred_element_type=F32)
        r = r + jnp.dot(a[:, 512:], wp[j, :, cols], preferred_element_type=F32)
        keep[n] = r[:192].reshape(2, 96, NC)
        xs[n, 0] = r[192:288].astype(BF16)
        xs[n, 1] = r[288:].astype(BF16)
        start(rcopy(xs.at[n, 0], xr.at[n, 0], x_s.at[n, 0], x_r.at[n, 0], xup))
        start(rcopy(xs.at[n, 1], xr.at[n, 1], x_s.at[n, 1], x_r.at[n, 1], xdn))

    from_below = lax.rem(x + 3, 4) // 2

    def reduce_x(n):
        for d in range(2):
            rcopy(xs.at[n, d], xr.at[n, d], x_s.at[n, d], x_r.at[n, d], xup).wait_recv()
        far = 1 - zh
        keep[n, zh] = keep[n, zh] + xr[n, (zh + from_below) % 2].astype(F32)
        zs[n] = (keep[n, far] + xr[n, (far + from_below) % 2].astype(F32)).astype(BF16)
        start(rcopy(zs.at[n], zr.at[n], z_s.at[n], z_r.at[n], hdev))

    def reduce_z(n):
        rcopy(zs.at[n], zr.at[n], z_s.at[n], z_r.at[n], hdev).wait_recv()
        total = (keep[n, zh] + zr[n].astype(F32)).astype(BF16)
        col = pl.multiple_of(order[n // 4] * 1024 + n % 4 * NC, NC)
        out[:, pl.ds(col, NC)] = total[:48]
        out[:, pl.ds(4096 + col, NC)] = total[48:]

    for n in range(4):
        matmul(n)
    for n in range(16):
        reduce_x(n)
        if n + 4 < 16:
            matmul(n + 4)
        if n >= 3:
            reduce_z(n - 3)
    for n in (13, 14, 15):
        reduce_z(n)
    for cp in sends:
        cp.wait_send()


def vmem():
    return pl.BlockSpec(memory_space=pltpu.VMEM)


def anyspace():
    return pl.BlockSpec(memory_space=pl.ANY)


def shards(activations, noise_mask, span_order, mask_vector, input_weights, output_weight):
    dma = pltpu.SemaphoreType.DMA
    return pl.pallas_call(
        kernel,
        out_shape=jax.ShapeDtypeStruct((48, 8192), BF16),
        in_specs=[pl.BlockSpec(memory_space=pltpu.SMEM), anyspace(), vmem(), vmem(), anyspace(), anyspace()],
        out_specs=vmem(),
        scratch_shapes=[
            pltpu.VMEM((ROWS + 16, 4096), BF16),
            pltpu.VMEM((3, 4096, 512), BF16),
            pltpu.VMEM((3, 4, ROWS + 16, HEAD), BF16),
            pltpu.VMEM((16, 2, ROWS, HEAD), BF16),
            pltpu.VMEM((4, ROWS, HEAD), BF16),
            pltpu.VMEM((4, 8, ROWS), F32),
            pltpu.VMEM((8, QT, HEAD), BF16),
            pltpu.VMEM((8, QT, HEAD), F32),
            pltpu.VMEM((8, QT, 2 * HEAD), F32),
            pltpu.VMEM((4, 8, 96, HEAD), BF16),
            pltpu.VMEM((4, 96, 1024), BF16),
            pltpu.VMEM((4, 512, 1024), BF16),
            pltpu.VMEM((4, 512, 1024), BF16),
            pltpu.VMEM((16, 2, 96, NC), F32),
            pltpu.VMEM((16, 2, 96, NC), BF16),
            pltpu.VMEM((16, 2, 96, NC), BF16),
            pltpu.VMEM((16, 96, NC), BF16),
            pltpu.VMEM((16, 96, NC), BF16),
            dma((4,)),
            dma((6,)),
            dma((4,)),
            dma,
            dma((2, 4)),
            dma((2, 16)),
            dma((16,)),
            dma((4,)),
            dma((4,)),
            dma((4,)),
            dma((4,)),
            dma((2,)),
            dma((2,)),
            dma((8,)),
            dma((8,)),
            dma((8,)),
            dma((2,)),
            dma((2,)),
            dma((2,)),
            dma((2,)),
            dma((2,)),
            dma((2,)),
            dma((2,)),
            dma((2,)),
            dma((16, 2)),
            dma((16, 2)),
            dma((16,)),
            dma((16,)),
        ],
        compiler_params=pltpu.CompilerParams(
            collective_id=1, has_side_effects=True, vmem_limit_bytes=VMEM_BYTES
        ),
        name="whole",
    )(
        span_order,
        activations,
        noise_mask,
        mask_vector,
        input_weights,
        output_weight,
    )


def solution(mesh):
    in_specs = (P("ctx", None), P("ctx"), P(), P(), P(None, None, "head"), P("head", None))
    out_specs = P(("ctx", "head"), None)
    return jax.shard_map(shards, mesh=mesh, in_specs=in_specs, out_specs=out_specs, check_vma=False)
```

```python
import functools
import math

import jax
import jax.numpy as jnp
from jax import lax
from jax.experimental import pallas as pl
from jax.experimental.pallas import tpu as pltpu
from jax.sharding import PartitionSpec as P

MESH = pl.DeviceIdType.MESH
HEAD = 128
ROWS = 384
HALF = 192
BLOCK = 64
QT = 208
NEG = -1e30
VMEM_BYTES = 60 << 20
NC = 256
LOG2_SCALE = math.log2(math.e) / math.sqrt(HEAD)
F32 = jnp.float32
BF16 = jnp.bfloat16


def coords():
    i = lax.axis_index("ctx")
    j = lax.axis_index("head")
    return j // 2, i // 4, (i // 2) % 2, j % 2, i % 2


def ctx_of(y, zl, c):
    return (y * 2 + zl) * 2 + c


def rcopy(src, dst, ssem, rsem, dev):
    return pltpu.make_async_remote_copy(
        src_ref=src, dst_ref=dst, send_sem=ssem, recv_sem=rsem, device_id=dev, device_id_type=MESH
    )


def greet(devs):
    barrier = pltpu.get_barrier_semaphore()
    for dev in devs:
        pl.semaphore_signal(barrier, inc=1, device_id=dev, device_id_type=MESH)
    return lambda: pl.semaphore_wait(barrier, len(devs))


def kernel(
    span, act, nmask, mvec, w, wo, out,
    lhs, wbuf, st, kv, q, msk, qt, m_ref, o_ref, mc_ref, oc_ref, mn_ref, on_ref, att, abuf, wown, wp, keep, xs, xr, zs, zr,
    act_l, w_l, wo_l, own_l, f_s, f_r, g_r, q_s, q_r, m_s, m_r, zk_s, zf_s, c_s, a_s, a_r,
    wx_s, wx_r, wc_s, wc_r, wy_s, wy_r, wf_s, wf_r, x_s, x_r, z_s, z_r,
):
    x, y, zl, zh, c = coords()
    hd = lax.axis_index("head")
    me = ctx_of(y, zl, c)
    ys = [y] + [lax.rem(y + k, 4) for k in (1, 2, 3)]
    x2 = lax.rem(x + 2, 4)
    ydev = [(ctx_of(ys[k], zl, c), hd) for k in range(4)]
    adev = [ydev, [(ctx_of(ys[k], zl, c), x2 * 2 + zh) for k in range(4)]]
    zdev = (ctx_of(y, 1 - zl, c), hd)
    ddev = (ctx_of(ys[2], 1 - zl, c), hd)
    cdev = (ctx_of(y, zl, 1 - c), hd)
    xup = (me, lax.rem(x + 1, 4) * 2 + zh)
    xdn = (me, lax.rem(x + 3, 4) * 2 + zh)
    hdev = (me, x * 2 + 1 - zh)
    wydev = (ctx_of(lax.rem(y + 1 + 2 * c, 4), zl, c), hd)
    arrive = greet(ydev[1:] + adev[1] + [zdev, ddev, cdev, xup, xdn, hdev])

    sends = []

    def start(cp):
        cp.start()
        sends.append(cp)

    loads = []
    for kc in range(4):
        part = pl.ds(kc * 1024, 1024)
        loads.append(
            (
                pltpu.make_async_copy(act.at[:, part], lhs.at[pl.ds(0, ROWS), part], act_l.at[kc]),
                pltpu.make_async_copy(w.at[0, part], wbuf.at[0, part], w_l.at[kc]),
            )
        )
    wk = pltpu.make_async_copy(w.at[1], wbuf.at[1], w_l.at[4])
    wv = pltpu.make_async_copy(w.at[2], wbuf.at[2], w_l.at[5])
    qd = lax.rem(y, 2) * 2 + c
    order = (qd, qd + 1 - 2 * c, lax.rem(qd + 2, 4), lax.rem(qd + 2, 4) + 1 - 2 * c)
    wol = []
    for n in range(4):
        col = pl.multiple_of(order[n] * 1024, 1024)
        wol.append(pltpu.make_async_copy(wo.at[:, pl.ds(col, 1024)], wown.at[n], wo_l.at[n]))

    def load(*copies):
        for cp in copies:
            cp.start()

    load(*loads[0], *loads[1], *loads[2])
    lhs[pl.ds(ROWS, 16), :] = jnp.broadcast_to(mvec[...].reshape(1, 4096), (16, 4096))
    msk[y] = jnp.broadcast_to(nmask[...].astype(F32).reshape(1, ROWS), (8, ROWS))

    def keep_heads(m, r):
        for j in range(4):
            st[m, j] = r[:, j * HEAD : (j + 1) * HEAD].astype(BF16)

    arrive()
    for e in range(2):
        col = pl.multiple_of(qd * 1024 + e * 512, 512)
        half = wp.at[0, :, pl.ds(e * 512, 512)]
        start(rcopy(wo.at[:, pl.ds(col, 512)], half, wx_s.at[e], wx_r.at[e], adev[1][0]))

    rows = pl.ds(0, ROWS)
    r = None
    for kc in range(4):
        for cp in loads[kc]:
            cp.wait()
        if kc == 0:
            load(*loads[3])
        if kc == 1:
            load(wk)
        part = pl.ds(kc * 1024, 1024)
        d = jnp.dot(lhs[:, part], wbuf[0, part], preferred_element_type=F32)
        r = d if r is None else r + d
    load(wv)
    keep_heads(0, r * LOG2_SCALE)
    for k in (1, 3, 2):
        start(rcopy(st.at[0, ys[k], rows], q.at[y], q_s.at[k], q_r.at[y], ydev[k]))
        start(rcopy(msk.at[y], msk.at[y], m_s.at[k], m_r.at[y], ydev[k]))
    q[y] = st[0, y, rows]

    for m, cp in ((1, wk), (2, wv)):
        cp.wait()
        if m == 2:
            load(*wol)
        keep_heads(m, jnp.dot(lhs[...], wbuf[m], preferred_element_type=F32))
        dst = kv.at[me, m - 1]
        start(rcopy(st.at[m, y, rows], dst, zk_s.at[m - 1], f_r.at[m - 1, me], zdev))
        for k in (1, 3):
            start(rcopy(st.at[m, ys[k], rows], dst, f_s.at[m - 1, k], f_r.at[m - 1, me], ydev[k]))
        kv[me, m - 1] = st[m, y, rows]
    start(rcopy(kv.at[me], kv.at[me], c_s.at[0], g_r.at[me], cdev))
    def here(k, z, split):
        slot = ctx_of(ys[k], z, c)
        if split:
            for m in range(2):
                rcopy(kv.at[slot, m], kv.at[slot, m], zk_s.at[m], f_r.at[m, slot], cdev).wait_recv()
        else:
            rcopy(kv.at[slot], kv.at[slot], zk_s.at[0], g_r.at[slot], cdev).wait_recv()
        return slot

    def to_core(n, slot):
        start(rcopy(kv.at[slot], kv.at[slot], c_s.at[n], g_r.at[slot], cdev))

    def to_z(n, slot):
        start(rcopy(kv.at[slot], kv.at[slot], zf_s.at[n], g_r.at[slot], zdev))

    def from_core(k, z):
        slot = ctx_of(ys[k], z, 1 - c)
        rcopy(kv.at[slot], kv.at[slot], zk_s.at[0], g_r.at[slot], cdev).wait_recv()

    def send_wp(e):
        half = wp.at[0, :, pl.ds(e * 512, 512)]
        rcopy(half, half, wx_s.at[e], wx_r.at[e], cdev).wait_recv()
        start(rcopy(half, wp.at[1, :, pl.ds(e * 512, 512)], wc_s.at[e], wc_r.at[e], cdev))
        start(rcopy(half, wp.at[2, :, pl.ds(e * 512, 512)], wy_s.at[e], wy_r.at[e], wydev))

    def chunk(pa, pb):
        place = lax.broadcasted_iota(jnp.int32, (1, 4 * ROWS), 1) // HALF
        ks = jnp.zeros((1, 4 * ROWS), jnp.int32)
        for n in range(8):
            ks = jnp.where(place == n, span[4 * (pa if n < 4 else pb) + n % 4], ks)
        refs = [(p, m) for m in range(2) for p in (pa, pb)]
        got = [kv[pl.ds(2 * p, 2), m].reshape(2 * ROWS, HEAD) for p, m in refs]
        k = jnp.concatenate(got[:2], axis=0)
        v = jnp.concatenate(got[2:], axis=0)
        return k, jnp.concatenate([v, jnp.ones((4 * ROWS, HEAD), BF16)], axis=1), ks

    def attend(i, u, keys, first):
        k, v, ks = keys
        sc = lax.dot_general(qt[i], k, (((1,), (1,)), ((), ())), preferred_element_type=F32)
        sc = sc + jnp.where(ks < u, F32(0), F32(NEG))
        top = jnp.max(sc, axis=1, keepdims=True)
        if first:
            new = jnp.maximum(top, F32(NEG))
        else:
            old = m_ref[i][:, :1]
            new = jnp.maximum(old, top)
        p = jnp.exp2(sc - new).astype(BF16)
        o = jnp.dot(p, v, preferred_element_type=F32)
        if not first:
            o = o_ref[i] * jnp.exp2(old - new) + o
        return new, o

    def step(pa, pb, first):
        keys = chunk(pa, pb)
        for i in range(8):
            u = span[2 * ctx_of(i // 2, zl, c) + i % 2]
            new, o = attend(i, u, keys, first)
            m_ref[i] = jnp.broadcast_to(new, (QT, HEAD))
            o_ref[i] = o

    def pair(k, z):
        return ys[k] * 2 + z

    p_x = x // 2
    rowi = lax.broadcasted_iota(jnp.int32, (QT, HALF), 0)
    coli = lax.broadcasted_iota(jnp.int32, (QT, HALF), 1)
    bi = jnp.where(rowi < HALF, rowi // BLOCK, jnp.minimum(rowi - HALF, 2))
    bj = coli // BLOCK

    def own_keys(s):
        km = st[1, y, pl.ds(ROWS, 16), :]
        vm = st[2, y, pl.ds(ROWS, 16), :][:1].astype(F32)
        vm = jnp.concatenate([vm, jnp.ones((1, HEAD), F32)], axis=1)
        src = ctx_of(s, zl, c)
        for h in range(2):
            i = 2 * s + h
            qi = jnp.concatenate([q[s, pl.ds(h * HALF, HALF), :], st[0, y, pl.ds(ROWS, 16), :]], axis=0)
            ko = kv[src, 0, pl.ds(h * HALF, HALF), :]
            vo = kv[src, 1, pl.ds(h * HALF, HALF), :]
            vo = jnp.concatenate([vo, jnp.ones((HALF, HEAD), BF16)], axis=1)
            so = lax.dot_general(qi, ko, (((1,), (1,)), ((), ())), preferred_element_type=F32)
            sm = lax.dot_general(qi, km, (((1,), (1,)), ((), ())), preferred_element_type=F32)[:, :1]
            mrow = msk[s, pl.ds(0, 1), pl.ds(h * HALF, HALF)]
            sc = jnp.where(bj <= bi, so, F32(NEG))
            mc = jnp.max(sc, axis=1, keepdims=True)
            pc = jnp.exp2(sc - mc).astype(BF16)
            mc_ref[i] = jnp.broadcast_to(mc, (QT, HEAD))
            oc_ref[i] = jnp.dot(pc, vo, preferred_element_type=F32)
            hit = (bj == bi) & (mrow > 0.5)
            sn = jnp.where(hit, sm, sc)
            mn = jnp.max(sn, axis=1, keepdims=True)
            pn = jnp.exp2(sn - mn).astype(BF16).astype(F32)
            pz = jnp.where(hit, F32(0), pn)
            wm = jnp.sum(pn - pz, axis=1, keepdims=True)
            mn_ref[i] = jnp.broadcast_to(mn, (QT, HEAD))
            on_ref[i] = jnp.dot(pz.astype(BF16), vo, preferred_element_type=F32) + wm * vm

    for h in range(2):
        qt[2 * y + h, pl.ds(0, HALF), :] = q[y, pl.ds(h * HALF, HALF), :]
        qt[2 * y + h, pl.ds(HALF, 16), :] = st[0, y, pl.ds(ROWS, 16), :]
    own_keys(y)
    to_core(1, here(0, 1 - zl, True))
    for n, k in ((0, 1), (1, 3)):
        slot = here(k, zl, True)
        to_z(n, slot)
        to_core(2 + n, slot)
    for m in (1, 2):
        dst = kv.at[me, m - 1]
        start(rcopy(st.at[m, ys[2], rows], dst, f_s.at[m - 1, 2], f_r.at[m - 1, me], ydev[2]))
        start(rcopy(st.at[m, ys[2], rows], dst, f_s.at[m - 1, 0], f_r.at[m - 1, me], ddev))
    for k in (1, 3, 2):
        rcopy(q.at[ys[k]], q.at[ys[k]], q_s.at[1], q_r.at[ys[k]], cdev).wait_recv()
        rcopy(msk.at[ys[k]], msk.at[ys[k]], m_s.at[1], m_r.at[ys[k]], cdev).wait_recv()
    for k in (1, 3, 2):
        for h in range(2):
            qt[2 * ys[k] + h, pl.ds(0, HALF), :] = q[ys[k], pl.ds(h * HALF, HALF), :]
            qt[2 * ys[k] + h, pl.ds(HALF, 16), :] = st[0, y, pl.ds(ROWS, 16), :]
    from_core(0, zl)
    from_core(0, 1 - zl)
    step(pair(0, zl), pair(0, 1 - zl), True)
    own_keys(ys[1])
    own_keys(ys[3])
    from_core(1, zl)
    from_core(3, zl)
    step(pair(1, zl), pair(3, zl), False)
    to_core(4, here(2, zl, True))
    to_core(5, here(1, 1 - zl, False))
    send_wp(0)
    own_keys(ys[2])
    from_core(2, zl)
    from_core(1, 1 - zl)
    step(pair(2, zl), pair(1, 1 - zl), False)
    to_core(6, here(3, 1 - zl, False))
    to_core(7, here(2, 1 - zl, True))
    send_wp(1)
    from_core(3, 1 - zl)
    from_core(2, 1 - zl)

    def join(mp, op, mo, oo):
        top = jnp.maximum(mp, mo)
        o = op * jnp.exp2(mp - top) + oo * jnp.exp2(mo - top)
        return o[:, :HEAD] / o[:, HEAD:]

    def finish(s, h, mp, op):
        i = 2 * s + h
        mrow = msk[s, pl.ds(0, 1), pl.ds(h * HALF, HALF)]
        clean = join(mp, op, mc_ref[i][:, :1], oc_ref[i])[:HALF].astype(BF16)
        an = join(mp, op, mn_ref[i][:, :1], on_ref[i])
        mcol = jnp.sum(jnp.where(rowi == coli, mrow, F32(0)), axis=1, keepdims=True)[:HALF]
        masked = jnp.concatenate(
            [jnp.broadcast_to(an[HALF + b : HALF + b + 1], (BLOCK, HEAD)) for b in range(3)], axis=0
        )
        noisy = jnp.where(mcol > 0.5, masked, an[:HALF]).astype(BF16)

        for b in range(4):
            xo = 2 * h + b // 2
            zo = b % 2
            near = zo == p_x
            side = jnp.where(near, lax.rem(x + 1, 4), lax.rem(x + 3, 4))
            pos = jnp.where(
                xo == x,
                zo,
                jnp.where(xo == x2, 4 + zo, jnp.where(near, 0, 4) + jnp.where(xo == side, 2, 3)),
            )
            att[s, pos, pl.ds(0, 48), :] = clean[b * 48 : (b + 1) * 48]
            att[s, pos, pl.ds(48, 48), :] = noisy[b * 48 : (b + 1) * 48]

    last = chunk(pair(3, 1 - zl), pair(2, 1 - zl))
    own = None
    for group in ((2, 1), (3, 0)):
        done = [
            [attend(2 * ys[k] + h, span[2 * ctx_of(ys[k], zl, c) + h], last, False) for h in range(2)]
            for k in group
        ]
        for k, parts in zip(group, done):
            s = ys[k]
            for h in range(2):
                finish(s, h, *parts[h])
            for t in (1, 0):
                dst = abuf.at[:, :, pl.ds(pl.multiple_of((4 * t + y) * HEAD, HEAD), HEAD)]
                if (t, k) == (0, 0):
                    own = pltpu.make_async_copy(att.at[s, pl.ds(0, 4)], dst, own_l)
                    own.start()
                else:
                    start(
                        rcopy(att.at[s, pl.ds(4 * t, 4)], dst, a_s.at[4 * t + k], a_r.at[4 * t + y], adev[t][k])
                    )
    own.wait()
    for t, k in ((0, 2), (1, 2), (0, 1), (1, 1), (0, 3), (1, 3), (1, 0)):
        slot = 4 * t + ys[k]
        dst = abuf.at[:, :, pl.ds(pl.multiple_of(slot * HEAD, HEAD), HEAD)]
        rcopy(att.at[0, pl.ds(0, 4)], dst, a_s.at[1], a_r.at[slot], cdev).wait_recv()

    def matmul(n):
        j, e = n // 4, n // 2 % 2
        if n % 4 == 0:
            wol[j].wait()
        half = wp.at[j, :, pl.ds(e * 512, 512)]
        if n % 2 == 0 and j == 1:
            rcopy(half, half, wc_s.at[e], wc_r.at[e], cdev).wait_recv()
        if n % 2 == 0 and j == 2:
            rcopy(half, half, wy_s.at[e], wy_r.at[e], cdev).wait_recv()
            start(rcopy(half, wp.at[3, :, pl.ds(e * 512, 512)], wf_s.at[e], wf_r.at[e], cdev))
        if n % 2 == 0 and j == 3:
            rcopy(half, half, wf_s.at[e], wf_r.at[e], cdev).wait_recv()
        cols = pl.ds(n % 4 * NC, NC)
        a = abuf[...].reshape(ROWS, 1024)
        r = jnp.dot(a[:, :512], wown[j, :, cols], preferred_element_type=F32)
        r = r + jnp.dot(a[:, 512:], wp[j, :, cols], preferred_element_type=F32)
        keep[n] = r[:192].reshape(2, 96, NC)
        xs[n, 0] = r[192:288].astype(BF16)
        xs[n, 1] = r[288:].astype(BF16)
        start(rcopy(xs.at[n, 0], xr.at[n, 0], x_s.at[n, 0], x_r.at[n, 0], xup))
        start(rcopy(xs.at[n, 1], xr.at[n, 1], x_s.at[n, 1], x_r.at[n, 1], xdn))

    from_below = lax.rem(x + 3, 4) // 2

    def reduce_x(n):
        for d in range(2):
            rcopy(xs.at[n, d], xr.at[n, d], x_s.at[n, d], x_r.at[n, d], xup).wait_recv()
        far = 1 - zh
        keep[n, zh] = keep[n, zh] + xr[n, (zh + from_below) % 2].astype(F32)
        zs[n] = (keep[n, far] + xr[n, (far + from_below) % 2].astype(F32)).astype(BF16)
        start(rcopy(zs.at[n], zr.at[n], z_s.at[n], z_r.at[n], hdev))

    def reduce_z(n):
        rcopy(zs.at[n], zr.at[n], z_s.at[n], z_r.at[n], hdev).wait_recv()
        total = (keep[n, zh] + zr[n].astype(F32)).astype(BF16)
        col = pl.multiple_of(order[n // 4] * 1024 + n % 4 * NC, NC)
        out[:, pl.ds(col, NC)] = total[:48]
        out[:, pl.ds(4096 + col, NC)] = total[48:]

    for n in range(4):
        matmul(n)
    for n in range(16):
        reduce_x(n)
        if n + 4 < 16:
            matmul(n + 4)
        if n >= 3:
            reduce_z(n - 3)
    for n in (13, 14, 15):
        reduce_z(n)
    for cp in sends:
        cp.wait_send()


def vmem():
    return pl.BlockSpec(memory_space=pltpu.VMEM)


def anyspace():
    return pl.BlockSpec(memory_space=pl.ANY)


def shards(activations, noise_mask, span_order, mask_vector, input_weights, output_weight):
    dma = pltpu.SemaphoreType.DMA
    return pl.pallas_call(
        kernel,
        out_shape=jax.ShapeDtypeStruct((48, 8192), BF16),
        in_specs=[pl.BlockSpec(memory_space=pltpu.SMEM), anyspace(), vmem(), vmem(), anyspace(), anyspace()],
        out_specs=vmem(),
        scratch_shapes=[
            pltpu.VMEM((ROWS + 16, 4096), BF16),
            pltpu.VMEM((3, 4096, 512), BF16),
            pltpu.VMEM((3, 4, ROWS + 16, HEAD), BF16),
            pltpu.VMEM((16, 2, ROWS, HEAD), BF16),
            pltpu.VMEM((4, ROWS, HEAD), BF16),
            pltpu.VMEM((4, 8, ROWS), F32),
            pltpu.VMEM((8, QT, HEAD), BF16),
            pltpu.VMEM((8, QT, HEAD), F32),
            pltpu.VMEM((8, QT, 2 * HEAD), F32),
            pltpu.VMEM((8, QT, HEAD), F32),
            pltpu.VMEM((8, QT, 2 * HEAD), F32),
            pltpu.VMEM((8, QT, HEAD), F32),
            pltpu.VMEM((8, QT, 2 * HEAD), F32),
            pltpu.VMEM((4, 8, 96, HEAD), BF16),
            pltpu.VMEM((4, 96, 1024), BF16),
            pltpu.VMEM((4, 512, 1024), BF16),
            pltpu.VMEM((4, 512, 1024), BF16),
            pltpu.VMEM((16, 2, 96, NC), F32),
            pltpu.VMEM((16, 2, 96, NC), BF16),
            pltpu.VMEM((16, 2, 96, NC), BF16),
            pltpu.VMEM((16, 96, NC), BF16),
            pltpu.VMEM((16, 96, NC), BF16),
            dma((4,)),
            dma((6,)),
            dma((4,)),
            dma,
            dma((2, 4)),
            dma((2, 16)),
            dma((16,)),
            dma((4,)),
            dma((4,)),
            dma((4,)),
            dma((4,)),
            dma((2,)),
            dma((2,)),
            dma((8,)),
            dma((8,)),
            dma((8,)),
            dma((2,)),
            dma((2,)),
            dma((2,)),
            dma((2,)),
            dma((2,)),
            dma((2,)),
            dma((2,)),
            dma((2,)),
            dma((16, 2)),
            dma((16, 2)),
            dma((16,)),
            dma((16,)),
        ],
        compiler_params=pltpu.CompilerParams(
            collective_id=1, has_side_effects=True, vmem_limit_bytes=VMEM_BYTES
        ),
        name="whole",
    )(
        span_order,
        activations,
        noise_mask,
        mask_vector,
        input_weights,
        output_weight,
    )


def solution(mesh):
    in_specs = (P("ctx", None), P("ctx"), P(), P(), P(None, None, "head"), P("head", None))
    out_specs = P(("ctx", "head"), None)
    return jax.shard_map(shards, mesh=mesh, in_specs=in_specs, out_specs=out_specs, check_vma=False)
```

```python
import functools
import math

import jax
import jax.numpy as jnp
from jax import lax
from jax.experimental import pallas as pl
from jax.experimental.pallas import tpu as pltpu
from jax.sharding import PartitionSpec as P

MESH = pl.DeviceIdType.MESH
HEAD = 128
ROWS = 384
HALF = 192
BLOCK = 64
QT = 208
NEG = -1e30
VMEM_BYTES = 52 << 20
NC = 256
LOG2_SCALE = math.log2(math.e) / math.sqrt(HEAD)
F32 = jnp.float32
BF16 = jnp.bfloat16


def coords():
    i = lax.axis_index("ctx")
    j = lax.axis_index("head")
    return j // 2, i // 4, (i // 2) % 2, j % 2, i % 2


def ctx_of(y, zl, c):
    return (y * 2 + zl) * 2 + c


def rcopy(src, dst, ssem, rsem, dev):
    return pltpu.make_async_remote_copy(
        src_ref=src, dst_ref=dst, send_sem=ssem, recv_sem=rsem, device_id=dev, device_id_type=MESH
    )


def greet(devs):
    barrier = pltpu.get_barrier_semaphore()
    for dev in devs:
        pl.semaphore_signal(barrier, inc=1, device_id=dev, device_id_type=MESH)
    return lambda: pl.semaphore_wait(barrier, len(devs))


def kernel(
    span, act, nmask, mvec, w, wo, out,
    lhs, wbuf, st, kv, q, msk, qt, m_ref, o_ref, mc_ref, oc_ref, mn_ref, on_ref, att, abuf, wown, wp, keep, xs, xr, zs, zr,
    act_l, w_l, wo_l, own_l, f_s, f_r, g_r, q_s, q_r, m_s, m_r, zk_s, zf_s, c_s, a_s, a_r,
    wx_s, wx_r, wc_s, wc_r, wy_s, wy_r, wf_s, wf_r, x_s, x_r, z_s, z_r,
):
    x, y, zl, zh, c = coords()
    hd = lax.axis_index("head")
    me = ctx_of(y, zl, c)
    ys = [y] + [lax.rem(y + k, 4) for k in (1, 2, 3)]
    x2 = lax.rem(x + 2, 4)
    ydev = [(ctx_of(ys[k], zl, c), hd) for k in range(4)]
    adev = [ydev, [(ctx_of(ys[k], zl, c), x2 * 2 + zh) for k in range(4)]]
    zdev = (ctx_of(y, 1 - zl, c), hd)
    ddev = (ctx_of(ys[2], 1 - zl, c), hd)
    cdev = (ctx_of(y, zl, 1 - c), hd)
    xup = (me, lax.rem(x + 1, 4) * 2 + zh)
    xdn = (me, lax.rem(x + 3, 4) * 2 + zh)
    hdev = (me, x * 2 + 1 - zh)
    wydev = (ctx_of(lax.rem(y + 1 + 2 * c, 4), zl, c), hd)
    arrive = greet(ydev[1:] + adev[1] + [zdev, ddev, cdev, xup, xdn, hdev])

    sends = []

    def start(cp):
        cp.start()
        sends.append(cp)

    loads = []
    for kc in range(4):
        part = pl.ds(kc * 1024, 1024)
        loads.append(
            (
                pltpu.make_async_copy(act.at[:, part], lhs.at[pl.ds(0, ROWS), part], act_l.at[kc]),
                pltpu.make_async_copy(w.at[0, part], wbuf.at[0, part], w_l.at[kc]),
            )
        )
    wk = pltpu.make_async_copy(w.at[1], wbuf.at[1], w_l.at[4])
    wv = pltpu.make_async_copy(w.at[2], wbuf.at[2], w_l.at[5])
    qd = lax.rem(y, 2) * 2 + c
    order = (qd, qd + 1 - 2 * c, lax.rem(qd + 2, 4), lax.rem(qd + 2, 4) + 1 - 2 * c)
    wol = []
    for n in range(4):
        col = pl.multiple_of(order[n] * 1024, 1024)
        wol.append(pltpu.make_async_copy(wo.at[:, pl.ds(col, 1024)], wown.at[n], wo_l.at[n]))

    def load(*copies):
        for cp in copies:
            cp.start()

    load(*loads[0], *loads[1], *loads[2])
    lhs[pl.ds(ROWS, 16), :] = jnp.broadcast_to(mvec[...].reshape(1, 4096), (16, 4096))
    msk[y] = jnp.broadcast_to(nmask[...].astype(F32).reshape(1, ROWS), (8, ROWS))

    def keep_heads(m, r):
        for j in range(4):
            st[m, j] = r[:, j * HEAD : (j + 1) * HEAD].astype(BF16)

    arrive()
    for e in range(2):
        col = pl.multiple_of(qd * 1024 + e * 512, 512)
        half = wp.at[0, :, pl.ds(e * 512, 512)]
        start(rcopy(wo.at[:, pl.ds(col, 512)], half, wx_s.at[e], wx_r.at[e], adev[1][0]))

    rows = pl.ds(0, ROWS)
    r = None
    for kc in range(4):
        for cp in loads[kc]:
            cp.wait()
        if kc == 0:
            load(*loads[3])
        if kc == 1:
            load(wk)
        part = pl.ds(kc * 1024, 1024)
        d = jnp.dot(lhs[:, part], wbuf[0, part], preferred_element_type=F32)
        r = d if r is None else r + d
    load(wv)
    keep_heads(0, r * LOG2_SCALE)
    for k in (1, 3, 2):
        start(rcopy(st.at[0, ys[k], rows], q.at[y], q_s.at[k], q_r.at[y], ydev[k]))
        start(rcopy(msk.at[y], msk.at[y], m_s.at[k], m_r.at[y], ydev[k]))
    q[y] = st[0, y, rows]

    for m, cp in ((1, wk), (2, wv)):
        cp.wait()
        if m == 2:
            load(*wol)
        keep_heads(m, jnp.dot(lhs[...], wbuf[m], preferred_element_type=F32))
        dst = kv.at[me, m - 1]
        start(rcopy(st.at[m, y, rows], dst, zk_s.at[m - 1], f_r.at[m - 1, me], zdev))
        for k in (1, 3):
            start(rcopy(st.at[m, ys[k], rows], dst, f_s.at[m - 1, k], f_r.at[m - 1, me], ydev[k]))
        kv[me, m - 1] = st[m, y, rows]
    start(rcopy(kv.at[me], kv.at[me], c_s.at[0], g_r.at[me], cdev))
    for m in (1, 2):
        dst = kv.at[me, m - 1]
        start(rcopy(st.at[m, ys[2], rows], dst, f_s.at[m - 1, 2], f_r.at[m - 1, me], ydev[2]))
    def here(k, z, split):
        slot = ctx_of(ys[k], z, c)
        if split:
            for m in range(2):
                rcopy(kv.at[slot, m], kv.at[slot, m], zk_s.at[m], f_r.at[m, slot], cdev).wait_recv()
        else:
            rcopy(kv.at[slot], kv.at[slot], zk_s.at[0], g_r.at[slot], cdev).wait_recv()
        return slot

    def to_core(n, slot):
        start(rcopy(kv.at[slot], kv.at[slot], c_s.at[n], g_r.at[slot], cdev))

    def to_z(n, slot):
        start(rcopy(kv.at[slot], kv.at[slot], zf_s.at[n], g_r.at[slot], zdev))

    def from_core(k, z):
        slot = ctx_of(ys[k], z, 1 - c)
        rcopy(kv.at[slot], kv.at[slot], zk_s.at[0], g_r.at[slot], cdev).wait_recv()

    def send_wp(e):
        half = wp.at[0, :, pl.ds(e * 512, 512)]
        rcopy(half, half, wx_s.at[e], wx_r.at[e], cdev).wait_recv()
        start(rcopy(half, wp.at[1, :, pl.ds(e * 512, 512)], wc_s.at[e], wc_r.at[e], cdev))
        start(rcopy(half, wp.at[2, :, pl.ds(e * 512, 512)], wy_s.at[e], wy_r.at[e], wydev))

    def chunk(pa, pb):
        place = lax.broadcasted_iota(jnp.int32, (1, 4 * ROWS), 1) // HALF
        ks = jnp.zeros((1, 4 * ROWS), jnp.int32)
        for n in range(8):
            ks = jnp.where(place == n, span[4 * (pa if n < 4 else pb) + n % 4], ks)
        refs = [(p, m) for m in range(2) for p in (pa, pb)]
        got = [kv[pl.ds(2 * p, 2), m].reshape(2 * ROWS, HEAD) for p, m in refs]
        k = jnp.concatenate(got[:2], axis=0)
        v = jnp.concatenate(got[2:], axis=0)
        return k, jnp.concatenate([v, jnp.ones((4 * ROWS, HEAD), BF16)], axis=1), ks

    def attend(i, u, keys, first):
        k, v, ks = keys
        sc = lax.dot_general(qt[i], k, (((1,), (1,)), ((), ())), preferred_element_type=F32)
        sc = sc + jnp.where(ks < u, F32(0), F32(NEG))
        top = jnp.max(sc, axis=1, keepdims=True)
        if first:
            new = jnp.maximum(top, F32(NEG))
        else:
            old = m_ref[i][:, :1]
            new = jnp.maximum(old, top)
        p = jnp.exp2(sc - new).astype(BF16)
        o = jnp.dot(p, v, preferred_element_type=F32)
        if not first:
            o = o_ref[i] * jnp.exp2(old - new) + o
        return new, o

    def step(pa, pb, first):
        keys = chunk(pa, pb)
        for i in range(8):
            u = span[2 * ctx_of(i // 2, zl, c) + i % 2]
            new, o = attend(i, u, keys, first)
            m_ref[i] = jnp.broadcast_to(new, (QT, HEAD))
            o_ref[i] = o

    def pair(k, z):
        return ys[k] * 2 + z

    p_x = x // 2
    rowi = lax.broadcasted_iota(jnp.int32, (QT, HALF), 0)
    coli = lax.broadcasted_iota(jnp.int32, (QT, HALF), 1)
    bi = jnp.where(rowi < HALF, rowi // BLOCK, jnp.minimum(rowi - HALF, 2))
    bj = coli // BLOCK

    def own_keys(s):
        km = st[1, y, pl.ds(ROWS, 16), :]
        vm = st[2, y, pl.ds(ROWS, 16), :][:1].astype(F32)
        vm = jnp.concatenate([vm, jnp.ones((1, HEAD), F32)], axis=1)
        src = ctx_of(s, zl, c)
        for h in range(2):
            i = 2 * s + h
            qi = jnp.concatenate([q[s, pl.ds(h * HALF, HALF), :], st[0, y, pl.ds(ROWS, 16), :]], axis=0)
            ko = kv[src, 0, pl.ds(h * HALF, HALF), :]
            vo = kv[src, 1, pl.ds(h * HALF, HALF), :]
            vo = jnp.concatenate([vo, jnp.ones((HALF, HEAD), BF16)], axis=1)
            so = lax.dot_general(qi, ko, (((1,), (1,)), ((), ())), preferred_element_type=F32)
            sm = lax.dot_general(qi, km, (((1,), (1,)), ((), ())), preferred_element_type=F32)[:, :1]
            mrow = msk[s, pl.ds(0, 1), pl.ds(h * HALF, HALF)]
            sc = jnp.where(bj <= bi, so, F32(NEG))
            mc = jnp.max(sc, axis=1, keepdims=True)
            pc = jnp.exp2(sc - mc).astype(BF16)
            mc_ref[i] = jnp.broadcast_to(mc, (QT, HEAD))
            oc_ref[i] = jnp.dot(pc, vo, preferred_element_type=F32)
            hit = (bj == bi) & (mrow > 0.5)
            sn = jnp.where(hit, sm, sc)
            mn = jnp.max(sn, axis=1, keepdims=True)
            pn = jnp.exp2(sn - mn).astype(BF16).astype(F32)
            pz = jnp.where(hit, F32(0), pn)
            wm = jnp.sum(pn - pz, axis=1, keepdims=True)
            mn_ref[i] = jnp.broadcast_to(mn, (QT, HEAD))
            on_ref[i] = jnp.dot(pz.astype(BF16), vo, preferred_element_type=F32) + wm * vm

    for h in range(2):
        qt[2 * y + h, pl.ds(0, HALF), :] = q[y, pl.ds(h * HALF, HALF), :]
        qt[2 * y + h, pl.ds(HALF, 16), :] = st[0, y, pl.ds(ROWS, 16), :]
    own_keys(y)
    to_core(1, here(0, 1 - zl, True))
    for n, k in ((0, 1), (1, 3)):
        slot = here(k, zl, True)
        to_z(n, slot)
        to_core(2 + n, slot)
    for m in (1, 2):
        dst = kv.at[me, m - 1]
        start(rcopy(st.at[m, ys[2], rows], dst, f_s.at[m - 1, 0], f_r.at[m - 1, me], ddev))
    for k in (1, 3, 2):
        rcopy(q.at[ys[k]], q.at[ys[k]], q_s.at[1], q_r.at[ys[k]], cdev).wait_recv()
        rcopy(msk.at[ys[k]], msk.at[ys[k]], m_s.at[1], m_r.at[ys[k]], cdev).wait_recv()
    for k in (1, 3, 2):
        for h in range(2):
            qt[2 * ys[k] + h, pl.ds(0, HALF), :] = q[ys[k], pl.ds(h * HALF, HALF), :]
            qt[2 * ys[k] + h, pl.ds(HALF, 16), :] = st[0, y, pl.ds(ROWS, 16), :]
    from_core(0, zl)
    from_core(0, 1 - zl)
    step(pair(0, zl), pair(0, 1 - zl), True)
    own_keys(ys[1])
    own_keys(ys[3])
    from_core(1, zl)
    from_core(3, zl)
    step(pair(1, zl), pair(3, zl), False)
    to_core(4, here(2, zl, True))
    to_core(5, here(1, 1 - zl, False))
    own_keys(ys[2])
    from_core(2, zl)
    from_core(1, 1 - zl)
    step(pair(2, zl), pair(1, 1 - zl), False)
    to_core(6, here(3, 1 - zl, False))
    to_core(7, here(2, 1 - zl, True))
    from_core(3, 1 - zl)
    from_core(2, 1 - zl)

    def join(mp, op, mo, oo):
        top = jnp.maximum(mp, mo)
        o = op * jnp.exp2(mp - top) + oo * jnp.exp2(mo - top)
        return o[:, :HEAD] / o[:, HEAD:]

    def finish(s, h, mp, op):
        i = 2 * s + h
        mrow = msk[s, pl.ds(0, 1), pl.ds(h * HALF, HALF)]
        clean = join(mp, op, mc_ref[i][:, :1], oc_ref[i])[:HALF].astype(BF16)
        an = join(mp, op, mn_ref[i][:, :1], on_ref[i])
        mcol = jnp.sum(jnp.where(rowi == coli, mrow, F32(0)), axis=1, keepdims=True)[:HALF]
        masked = jnp.concatenate(
            [jnp.broadcast_to(an[HALF + b : HALF + b + 1], (BLOCK, HEAD)) for b in range(3)], axis=0
        )
        noisy = jnp.where(mcol > 0.5, masked, an[:HALF]).astype(BF16)

        for b in range(4):
            xo = 2 * h + b // 2
            zo = b % 2
            near = zo == p_x
            side = jnp.where(near, lax.rem(x + 1, 4), lax.rem(x + 3, 4))
            pos = jnp.where(
                xo == x,
                zo,
                jnp.where(xo == x2, 4 + zo, jnp.where(near, 0, 4) + jnp.where(xo == side, 2, 3)),
            )
            att[s, pos, pl.ds(0, 48), :] = clean[b * 48 : (b + 1) * 48]
            att[s, pos, pl.ds(48, 48), :] = noisy[b * 48 : (b + 1) * 48]

    send_wp(0)
    send_wp(1)
    last = chunk(pair(3, 1 - zl), pair(2, 1 - zl))
    own = None
    for group in ((2, 1), (3, 0)):
        done = [
            [attend(2 * ys[k] + h, span[2 * ctx_of(ys[k], zl, c) + h], last, False) for h in range(2)]
            for k in group
        ]
        for k, parts in zip(group, done):
            s = ys[k]
            for h in range(2):
                finish(s, h, *parts[h])
            for t in (1, 0):
                dst = abuf.at[:, :, pl.ds(pl.multiple_of((4 * t + y) * HEAD, HEAD), HEAD)]
                if (t, k) == (0, 0):
                    own = pltpu.make_async_copy(att.at[s, pl.ds(0, 4)], dst, own_l)
                    own.start()
                else:
                    start(
                        rcopy(att.at[s, pl.ds(4 * t, 4)], dst, a_s.at[4 * t + k], a_r.at[4 * t + y], adev[t][k])
                    )
    own.wait()
    for t, k in ((0, 2), (1, 2), (0, 1), (1, 1), (0, 3), (1, 3), (1, 0)):
        slot = 4 * t + ys[k]
        dst = abuf.at[:, :, pl.ds(pl.multiple_of(slot * HEAD, HEAD), HEAD)]
        rcopy(att.at[0, pl.ds(0, 4)], dst, a_s.at[1], a_r.at[slot], cdev).wait_recv()

    def matmul(n):
        j, e = n // 4, n // 2 % 2
        if n % 4 == 0:
            wol[j].wait()
        half = wp.at[j, :, pl.ds(e * 512, 512)]
        if n % 2 == 0 and j == 1:
            rcopy(half, half, wc_s.at[e], wc_r.at[e], cdev).wait_recv()
        if n % 2 == 0 and j == 2:
            rcopy(half, half, wy_s.at[e], wy_r.at[e], cdev).wait_recv()
            start(rcopy(half, wp.at[3, :, pl.ds(e * 512, 512)], wf_s.at[e], wf_r.at[e], cdev))
        if n % 2 == 0 and j == 3:
            rcopy(half, half, wf_s.at[e], wf_r.at[e], cdev).wait_recv()
        cols = pl.ds(n % 4 * NC, NC)
        a = abuf[...].reshape(ROWS, 1024)
        r = jnp.dot(a[:, :512], wown[j, :, cols], preferred_element_type=F32)
        r = r + jnp.dot(a[:, 512:], wp[j, :, cols], preferred_element_type=F32)
        keep[n] = r[:192].reshape(2, 96, NC)
        xs[n, 0] = r[192:288].astype(BF16)
        xs[n, 1] = r[288:].astype(BF16)
        start(rcopy(xs.at[n, 0], xr.at[n, 0], x_s.at[n, 0], x_r.at[n, 0], xup))
        start(rcopy(xs.at[n, 1], xr.at[n, 1], x_s.at[n, 1], x_r.at[n, 1], xdn))

    from_below = lax.rem(x + 3, 4) // 2

    def reduce_x(n):
        for d in range(2):
            rcopy(xs.at[n, d], xr.at[n, d], x_s.at[n, d], x_r.at[n, d], xup).wait_recv()
        far = 1 - zh
        keep[n, zh] = keep[n, zh] + xr[n, (zh + from_below) % 2].astype(F32)
        zs[n] = (keep[n, far] + xr[n, (far + from_below) % 2].astype(F32)).astype(BF16)
        start(rcopy(zs.at[n], zr.at[n], z_s.at[n], z_r.at[n], hdev))

    def reduce_z(n):
        rcopy(zs.at[n], zr.at[n], z_s.at[n], z_r.at[n], hdev).wait_recv()
        total = (keep[n, zh] + zr[n].astype(F32)).astype(BF16)
        col = pl.multiple_of(order[n // 4] * 1024 + n % 4 * NC, NC)
        out[:, pl.ds(col, NC)] = total[:48]
        out[:, pl.ds(4096 + col, NC)] = total[48:]

    for n in range(4):
        matmul(n)
    for n in range(16):
        reduce_x(n)
        if n + 4 < 16:
            matmul(n + 4)
        if n >= 3:
            reduce_z(n - 3)
    for n in (13, 14, 15):
        reduce_z(n)
    for cp in sends:
        cp.wait_send()


def vmem():
    return pl.BlockSpec(memory_space=pltpu.VMEM)


def anyspace():
    return pl.BlockSpec(memory_space=pl.ANY)


def shards(activations, noise_mask, span_order, mask_vector, input_weights, output_weight):
    dma = pltpu.SemaphoreType.DMA
    return pl.pallas_call(
        kernel,
        out_shape=jax.ShapeDtypeStruct((48, 8192), BF16),
        in_specs=[pl.BlockSpec(memory_space=pltpu.SMEM), anyspace(), vmem(), vmem(), anyspace(), anyspace()],
        out_specs=vmem(),
        scratch_shapes=[
            pltpu.VMEM((ROWS + 16, 4096), BF16),
            pltpu.VMEM((3, 4096, 512), BF16),
            pltpu.VMEM((3, 4, ROWS + 16, HEAD), BF16),
            pltpu.VMEM((16, 2, ROWS, HEAD), BF16),
            pltpu.VMEM((4, ROWS, HEAD), BF16),
            pltpu.VMEM((4, 8, ROWS), F32),
            pltpu.VMEM((8, QT, HEAD), BF16),
            pltpu.VMEM((8, QT, HEAD), F32),
            pltpu.VMEM((8, QT, 2 * HEAD), F32),
            pltpu.VMEM((8, QT, HEAD), F32),
            pltpu.VMEM((8, QT, 2 * HEAD), F32),
            pltpu.VMEM((8, QT, HEAD), F32),
            pltpu.VMEM((8, QT, 2 * HEAD), F32),
            pltpu.VMEM((4, 8, 96, HEAD), BF16),
            pltpu.VMEM((4, 96, 1024), BF16),
            pltpu.VMEM((4, 512, 1024), BF16),
            pltpu.VMEM((4, 512, 1024), BF16),
            pltpu.VMEM((16, 2, 96, NC), F32),
            pltpu.VMEM((16, 2, 96, NC), BF16),
            pltpu.VMEM((16, 2, 96, NC), BF16),
            pltpu.VMEM((16, 96, NC), BF16),
            pltpu.VMEM((16, 96, NC), BF16),
            dma((4,)),
            dma((6,)),
            dma((4,)),
            dma,
            dma((2, 4)),
            dma((2, 16)),
            dma((16,)),
            dma((4,)),
            dma((4,)),
            dma((4,)),
            dma((4,)),
            dma((2,)),
            dma((2,)),
            dma((8,)),
            dma((8,)),
            dma((8,)),
            dma((2,)),
            dma((2,)),
            dma((2,)),
            dma((2,)),
            dma((2,)),
            dma((2,)),
            dma((2,)),
            dma((2,)),
            dma((16, 2)),
            dma((16, 2)),
            dma((16,)),
            dma((16,)),
        ],
        compiler_params=pltpu.CompilerParams(
            collective_id=1, has_side_effects=True, vmem_limit_bytes=VMEM_BYTES
        ),
        name="whole",
    )(
        span_order,
        activations,
        noise_mask,
        mask_vector,
        input_weights,
        output_weight,
    )


def solution(mesh):
    in_specs = (P("ctx", None), P("ctx"), P(), P(), P(None, None, "head"), P("head", None))
    out_specs = P(("ctx", "head"), None)
    return jax.shard_map(shards, mesh=mesh, in_specs=in_specs, out_specs=out_specs, check_vma=False)
```

```python
import functools
import math

import jax
import jax.numpy as jnp
from jax import lax
from jax.experimental import pallas as pl
from jax.experimental.pallas import tpu as pltpu
from jax.sharding import PartitionSpec as P

MESH = pl.DeviceIdType.MESH
HEAD = 128
ROWS = 384
HALF = 192
BLOCK = 64
QT = 208
NEG = -1e30
VMEM_BYTES = 60 << 20
NC = 256
LOG2_SCALE = math.log2(math.e) / math.sqrt(HEAD)
F32 = jnp.float32
BF16 = jnp.bfloat16


def coords():
    i = lax.axis_index("ctx")
    j = lax.axis_index("head")
    return j // 2, i // 4, (i // 2) % 2, j % 2, i % 2


def ctx_of(y, zl, c):
    return (y * 2 + zl) * 2 + c


def rcopy(src, dst, ssem, rsem, dev):
    return pltpu.make_async_remote_copy(
        src_ref=src, dst_ref=dst, send_sem=ssem, recv_sem=rsem, device_id=dev, device_id_type=MESH
    )


def greet(devs):
    barrier = pltpu.get_barrier_semaphore()
    for dev in devs:
        pl.semaphore_signal(barrier, inc=1, device_id=dev, device_id_type=MESH)
    return lambda: pl.semaphore_wait(barrier, len(devs))


def kernel(
    span, act, nmask, mvec, w, wo, out,
    lhs, wbuf, st, kv, q, msk, qt, m_ref, o_ref, att, abuf, wown, wp, keep, xs, xr, zs, zr,
    act_l, w_l, wo_l, own_l, f_s, f_r, g_r, q_s, q_r, m_s, m_r, zk_s, zf_s, c_s, a_s, a_r,
    wx_s, wx_r, wc_s, wc_r, wy_s, wy_r, wf_s, wf_r, x_s, x_r, z_s, z_r,
):
    x, y, zl, zh, c = coords()
    hd = lax.axis_index("head")
    me = ctx_of(y, zl, c)
    ys = [y] + [lax.rem(y + k, 4) for k in (1, 2, 3)]
    x2 = lax.rem(x + 2, 4)
    ydev = [(ctx_of(ys[k], zl, c), hd) for k in range(4)]
    adev = [ydev, [(ctx_of(ys[k], zl, c), x2 * 2 + zh) for k in range(4)]]
    zdev = (ctx_of(y, 1 - zl, c), hd)
    ddev = (ctx_of(ys[2], 1 - zl, c), hd)
    cdev = (ctx_of(y, zl, 1 - c), hd)
    xup = (me, lax.rem(x + 1, 4) * 2 + zh)
    xdn = (me, lax.rem(x + 3, 4) * 2 + zh)
    hdev = (me, x * 2 + 1 - zh)
    wydev = (ctx_of(lax.rem(y + 1 + 2 * c, 4), zl, c), hd)
    arrive = greet(ydev[1:] + adev[1] + [zdev, ddev, cdev, xup, xdn, hdev])

    sends = []

    def start(cp):
        cp.start()
        sends.append(cp)

    loads = []
    for kc in range(4):
        part = pl.ds(kc * 1024, 1024)
        loads.append(
            (
                pltpu.make_async_copy(act.at[:, part], lhs.at[pl.ds(0, ROWS), part], act_l.at[kc]),
                pltpu.make_async_copy(w.at[0, part], wbuf.at[0, part], w_l.at[kc]),
            )
        )
    wk = pltpu.make_async_copy(w.at[1], wbuf.at[1], w_l.at[4])
    wv = pltpu.make_async_copy(w.at[2], wbuf.at[2], w_l.at[5])
    qd = lax.rem(y, 2) * 2 + c
    order = (qd, qd + 1 - 2 * c, lax.rem(qd + 2, 4), lax.rem(qd + 2, 4) + 1 - 2 * c)
    wol = []
    for n in range(4):
        col = pl.multiple_of(order[n] * 1024, 1024)
        wol.append(pltpu.make_async_copy(wo.at[:, pl.ds(col, 1024)], wown.at[n], wo_l.at[n]))

    def load(*copies):
        for cp in copies:
            cp.start()

    load(*loads[0], *loads[1], *loads[2])
    lhs[pl.ds(ROWS, 16), :] = jnp.broadcast_to(mvec[...].reshape(1, 4096), (16, 4096))
    msk[y] = jnp.broadcast_to(nmask[...].astype(F32).reshape(1, ROWS), (8, ROWS))

    def keep_heads(m, r):
        for j in range(4):
            st[m, j] = r[:, j * HEAD : (j + 1) * HEAD].astype(BF16)

    arrive()
    for e in range(2):
        col = pl.multiple_of(qd * 1024 + e * 512, 512)
        half = wp.at[0, :, pl.ds(e * 512, 512)]
        start(rcopy(wo.at[:, pl.ds(col, 512)], half, wx_s.at[e], wx_r.at[e], adev[1][0]))

    rows = pl.ds(0, ROWS)
    r = None
    for kc in range(4):
        for cp in loads[kc]:
            cp.wait()
        if kc == 0:
            load(*loads[3])
        if kc == 1:
            load(wk)
        part = pl.ds(kc * 1024, 1024)
        d = jnp.dot(lhs[:, part], wbuf[0, part], preferred_element_type=F32)
        r = d if r is None else r + d
    load(wv)
    keep_heads(0, r * LOG2_SCALE)
    for k in (1, 3, 2):
        start(rcopy(st.at[0, ys[k], rows], q.at[y], q_s.at[k], q_r.at[y], ydev[k]))
        start(rcopy(msk.at[y], msk.at[y], m_s.at[k], m_r.at[y], ydev[k]))
    q[y] = st[0, y, rows]

    for m, cp in ((1, wk), (2, wv)):
        cp.wait()
        if m == 2:
            load(*wol)
        keep_heads(m, jnp.dot(lhs[...], wbuf[m], preferred_element_type=F32))
        dst = kv.at[me, m - 1]
        start(rcopy(st.at[m, y, rows], dst, zk_s.at[m - 1], f_r.at[m - 1, me], zdev))
        for k in (1, 3):
            start(rcopy(st.at[m, ys[k], rows], dst, f_s.at[m - 1, k], f_r.at[m - 1, me], ydev[k]))
        kv[me, m - 1] = st[m, y, rows]
    start(rcopy(kv.at[me], kv.at[me], c_s.at[0], g_r.at[me], cdev))
    for m in (1, 2):
        dst = kv.at[me, m - 1]
        start(rcopy(st.at[m, ys[2], rows], dst, f_s.at[m - 1, 2], f_r.at[m - 1, me], ydev[2]))
        start(rcopy(st.at[m, ys[2], rows], dst, f_s.at[m - 1, 0], f_r.at[m - 1, me], ddev))
    def here(k, z, split):
        slot = ctx_of(ys[k], z, c)
        if split:
            for m in range(2):
                rcopy(kv.at[slot, m], kv.at[slot, m], zk_s.at[m], f_r.at[m, slot], cdev).wait_recv()
        else:
            rcopy(kv.at[slot], kv.at[slot], zk_s.at[0], g_r.at[slot], cdev).wait_recv()
        return slot

    def to_core(n, slot):
        start(rcopy(kv.at[slot], kv.at[slot], c_s.at[n], g_r.at[slot], cdev))

    def to_z(n, slot):
        start(rcopy(kv.at[slot], kv.at[slot], zf_s.at[n], g_r.at[slot], zdev))

    def from_core(k, z):
        slot = ctx_of(ys[k], z, 1 - c)
        rcopy(kv.at[slot], kv.at[slot], zk_s.at[0], g_r.at[slot], cdev).wait_recv()

    def send_wp(e):
        half = wp.at[0, :, pl.ds(e * 512, 512)]
        rcopy(half, half, wx_s.at[e], wx_r.at[e], cdev).wait_recv()
        start(rcopy(half, wp.at[1, :, pl.ds(e * 512, 512)], wc_s.at[e], wc_r.at[e], cdev))
        start(rcopy(half, wp.at[2, :, pl.ds(e * 512, 512)], wy_s.at[e], wy_r.at[e], wydev))

    def chunk(pa, pb):
        place = lax.broadcasted_iota(jnp.int32, (1, 4 * ROWS), 1) // HALF
        ks = jnp.zeros((1, 4 * ROWS), jnp.int32)
        for n in range(8):
            ks = jnp.where(place == n, span[4 * (pa if n < 4 else pb) + n % 4], ks)
        refs = [(p, m) for m in range(2) for p in (pa, pb)]
        got = [kv[pl.ds(2 * p, 2), m].reshape(2 * ROWS, HEAD) for p, m in refs]
        k = jnp.concatenate(got[:2], axis=0)
        v = jnp.concatenate(got[2:], axis=0)
        return k, jnp.concatenate([v, jnp.ones((4 * ROWS, HEAD), BF16)], axis=1), ks

    def attend(i, u, keys, first):
        k, v, ks = keys
        sc = lax.dot_general(qt[i], k, (((1,), (1,)), ((), ())), preferred_element_type=F32)
        sc = sc + jnp.where(ks < u, F32(0), F32(NEG))
        top = jnp.max(sc, axis=1, keepdims=True)
        if first:
            new = jnp.maximum(top, F32(NEG))
        else:
            old = m_ref[i][:, :1]
            new = jnp.maximum(old, top)
        p = jnp.exp2(sc - new).astype(BF16)
        o = jnp.dot(p, v, preferred_element_type=F32)
        if not first:
            o = o_ref[i] * jnp.exp2(old - new) + o
        return new, o

    def step(pa, pb, first):
        keys = chunk(pa, pb)
        for i in range(8):
            u = span[2 * ctx_of(i // 2, zl, c) + i % 2]
            new, o = attend(i, u, keys, first)
            m_ref[i] = jnp.broadcast_to(new, (QT, HEAD))
            o_ref[i] = o

    def pair(k, z):
        return ys[k] * 2 + z

    to_core(1, here(0, 1 - zl, True))
    for n, k in ((0, 1), (1, 3)):
        slot = here(k, zl, True)
        to_z(n, slot)
        to_core(2 + n, slot)
    for k in (1, 3, 2):
        rcopy(q.at[ys[k]], q.at[ys[k]], q_s.at[1], q_r.at[ys[k]], cdev).wait_recv()
        rcopy(msk.at[ys[k]], msk.at[ys[k]], m_s.at[1], m_r.at[ys[k]], cdev).wait_recv()
    for s in range(4):
        for h in range(2):
            qt[2 * s + h, pl.ds(0, HALF), :] = q[s, pl.ds(h * HALF, HALF), :]
            qt[2 * s + h, pl.ds(HALF, 16), :] = st[0, y, pl.ds(ROWS, 16), :]
    from_core(0, zl)
    from_core(0, 1 - zl)
    step(pair(0, zl), pair(0, 1 - zl), True)
    send_wp(0)
    from_core(1, zl)
    from_core(3, zl)
    step(pair(1, zl), pair(3, zl), False)
    to_core(4, here(2, zl, True))
    to_core(5, here(1, 1 - zl, False))
    from_core(2, zl)
    from_core(1, 1 - zl)
    step(pair(2, zl), pair(1, 1 - zl), False)
    to_core(6, here(3, 1 - zl, False))
    to_core(7, here(2, 1 - zl, True))
    send_wp(1)
    from_core(3, 1 - zl)
    from_core(2, 1 - zl)

    p_x = x // 2
    km = st[1, y, pl.ds(ROWS, 16), :]
    vm = st[2, y, pl.ds(ROWS, 16), :][:1].astype(F32)
    vm = jnp.concatenate([vm, jnp.ones((1, HEAD), F32)], axis=1)
    rowi = lax.broadcasted_iota(jnp.int32, (QT, HALF), 0)
    coli = lax.broadcasted_iota(jnp.int32, (QT, HALF), 1)
    bi = jnp.where(rowi < HALF, rowi // BLOCK, jnp.minimum(rowi - HALF, 2))
    bj = coli // BLOCK
    last = chunk(pair(3, 1 - zl), pair(2, 1 - zl))

    def finish(s, h):
        i = 2 * s + h
        src = ctx_of(s, zl, c)
        mp, op = attend(i, span[2 * src + h], last, False)
        qi = qt[i]
        ko = kv[src, 0, pl.ds(h * HALF, HALF), :]
        vo = jnp.concatenate([kv[src, 1, pl.ds(h * HALF, HALF), :], jnp.ones((HALF, HEAD), BF16)], axis=1)
        so = lax.dot_general(qi, ko, (((1,), (1,)), ((), ())), preferred_element_type=F32)
        sm = lax.dot_general(qi, km, (((1,), (1,)), ((), ())), preferred_element_type=F32)[:, :1]
        mrow = msk[s, pl.ds(0, 1), pl.ds(h * HALF, HALF)]

        sc = jnp.where(bj <= bi, so, F32(NEG))
        mc = jnp.maximum(mp, jnp.max(sc, axis=1, keepdims=True))
        pc = jnp.where(bj <= bi, jnp.exp2(sc - mc), F32(0)).astype(BF16)
        oc = op * jnp.exp2(mp - mc) + jnp.dot(pc, vo, preferred_element_type=F32)
        clean = (oc[:HALF, :HEAD] / oc[:HALF, HEAD:]).astype(BF16)

        hit = (bj == bi) & (mrow > 0.5)
        sn = jnp.where(hit, sm, sc)
        mn = jnp.maximum(mp, jnp.max(sn, axis=1, keepdims=True))
        pn = jnp.where(bj <= bi, jnp.exp2(sn - mn), F32(0)).astype(BF16)
        pz = jnp.where(hit, F32(0), pn.astype(F32))
        wm = jnp.sum(pn.astype(F32) - pz, axis=1, keepdims=True)
        on = op * jnp.exp2(mp - mn) + jnp.dot(pz.astype(BF16), vo, preferred_element_type=F32) + wm * vm
        an = on[:, :HEAD] / on[:, HEAD:]
        mcol = jnp.sum(jnp.where(rowi == coli, mrow, F32(0)), axis=1, keepdims=True)[:HALF]
        masked = jnp.concatenate(
            [jnp.broadcast_to(an[HALF + b : HALF + b + 1], (BLOCK, HEAD)) for b in range(3)], axis=0
        )
        noisy = jnp.where(mcol > 0.5, masked, an[:HALF]).astype(BF16)

        for b in range(4):
            xo = 2 * h + b // 2
            zo = b % 2
            near = zo == p_x
            side = jnp.where(near, lax.rem(x + 1, 4), lax.rem(x + 3, 4))
            pos = jnp.where(
                xo == x,
                zo,
                jnp.where(xo == x2, 4 + zo, jnp.where(near, 0, 4) + jnp.where(xo == side, 2, 3)),
            )
            att[s, pos, pl.ds(0, 48), :] = clean[b * 48 : (b + 1) * 48]
            att[s, pos, pl.ds(48, 48), :] = noisy[b * 48 : (b + 1) * 48]

    own = None
    for n, k in enumerate((2, 1, 3, 0)):
        s = ys[k]
        finish(s, 0)
        finish(s, 1)
        for t in (1, 0):
            dst = abuf.at[:, :, pl.ds(pl.multiple_of((4 * t + y) * HEAD, HEAD), HEAD)]
            if (t, k) == (0, 0):
                own = pltpu.make_async_copy(att.at[s, pl.ds(0, 4)], dst, own_l)
                own.start()
            else:
                start(rcopy(att.at[s, pl.ds(4 * t, 4)], dst, a_s.at[4 * t + k], a_r.at[4 * t + y], adev[t][k]))
    own.wait()
    for t, k in ((0, 2), (1, 2), (0, 1), (1, 1), (0, 3), (1, 3), (1, 0)):
        slot = 4 * t + ys[k]
        dst = abuf.at[:, :, pl.ds(pl.multiple_of(slot * HEAD, HEAD), HEAD)]
        rcopy(att.at[0, pl.ds(0, 4)], dst, a_s.at[1], a_r.at[slot], cdev).wait_recv()

    def matmul(n):
        j, e = n // 4, n // 2 % 2
        if n % 4 == 0:
            wol[j].wait()
        half = wp.at[j, :, pl.ds(e * 512, 512)]
        if n % 2 == 0 and j == 1:
            rcopy(half, half, wc_s.at[e], wc_r.at[e], cdev).wait_recv()
        if n % 2 == 0 and j == 2:
            rcopy(half, half, wy_s.at[e], wy_r.at[e], cdev).wait_recv()
            start(rcopy(half, wp.at[3, :, pl.ds(e * 512, 512)], wf_s.at[e], wf_r.at[e], cdev))
        if n % 2 == 0 and j == 3:
            rcopy(half, half, wf_s.at[e], wf_r.at[e], cdev).wait_recv()
        cols = pl.ds(n % 4 * NC, NC)
        a = abuf[...].reshape(ROWS, 1024)
        r = jnp.dot(a[:, :512], wown[j, :, cols], preferred_element_type=F32)
        r = r + jnp.dot(a[:, 512:], wp[j, :, cols], preferred_element_type=F32)
        keep[n] = r[:192].reshape(2, 96, NC)
        xs[n, 0] = r[192:288].astype(BF16)
        xs[n, 1] = r[288:].astype(BF16)
        start(rcopy(xs.at[n, 0], xr.at[n, 0], x_s.at[n, 0], x_r.at[n, 0], xup))
        start(rcopy(xs.at[n, 1], xr.at[n, 1], x_s.at[n, 1], x_r.at[n, 1], xdn))

    from_below = lax.rem(x + 3, 4) // 2

    def reduce_x(n):
        for d in range(2):
            rcopy(xs.at[n, d], xr.at[n, d], x_s.at[n, d], x_r.at[n, d], xup).wait_recv()
        far = 1 - zh
        keep[n, zh] = keep[n, zh] + xr[n, (zh + from_below) % 2].astype(F32)
        zs[n] = (keep[n, far] + xr[n, (far + from_below) % 2].astype(F32)).astype(BF16)
        start(rcopy(zs.at[n], zr.at[n], z_s.at[n], z_r.at[n], hdev))

    def reduce_z(n):
        rcopy(zs.at[n], zr.at[n], z_s.at[n], z_r.at[n], hdev).wait_recv()
        total = (keep[n, zh] + zr[n].astype(F32)).astype(BF16)
        col = pl.multiple_of(order[n // 4] * 1024 + n % 4 * NC, NC)
        out[:, pl.ds(col, NC)] = total[:48]
        out[:, pl.ds(4096 + col, NC)] = total[48:]

    for n in range(8):
        matmul(n)
    for n in range(16):
        reduce_x(n)
        if n + 8 < 16:
            matmul(n + 8)
        if n >= 6:
            reduce_z(n - 6)
    for n in range(10, 16):
        reduce_z(n)
    for cp in sends:
        cp.wait_send()


def vmem():
    return pl.BlockSpec(memory_space=pltpu.VMEM)


def anyspace():
    return pl.BlockSpec(memory_space=pl.ANY)


def shards(activations, noise_mask, span_order, mask_vector, input_weights, output_weight):
    dma = pltpu.SemaphoreType.DMA
    return pl.pallas_call(
        kernel,
        out_shape=jax.ShapeDtypeStruct((48, 8192), BF16),
        in_specs=[pl.BlockSpec(memory_space=pltpu.SMEM), anyspace(), vmem(), vmem(), anyspace(), anyspace()],
        out_specs=vmem(),
        scratch_shapes=[
            pltpu.VMEM((ROWS + 16, 4096), BF16),
            pltpu.VMEM((3, 4096, 512), BF16),
            pltpu.VMEM((3, 4, ROWS + 16, HEAD), BF16),
            pltpu.VMEM((16, 2, ROWS, HEAD), BF16),
            pltpu.VMEM((4, ROWS, HEAD), BF16),
            pltpu.VMEM((4, 8, ROWS), F32),
            pltpu.VMEM((8, QT, HEAD), BF16),
            pltpu.VMEM((8, QT, HEAD), F32),
            pltpu.VMEM((8, QT, 2 * HEAD), F32),
            pltpu.VMEM((4, 8, 96, HEAD), BF16),
            pltpu.VMEM((4, 96, 1024), BF16),
            pltpu.VMEM((4, 512, 1024), BF16),
            pltpu.VMEM((4, 512, 1024), BF16),
            pltpu.VMEM((16, 2, 96, NC), F32),
            pltpu.VMEM((16, 2, 96, NC), BF16),
            pltpu.VMEM((16, 2, 96, NC), BF16),
            pltpu.VMEM((16, 96, NC), BF16),
            pltpu.VMEM((16, 96, NC), BF16),
            dma((4,)),
            dma((6,)),
            dma((4,)),
            dma,
            dma((2, 4)),
            dma((2, 16)),
            dma((16,)),
            dma((4,)),
            dma((4,)),
            dma((4,)),
            dma((4,)),
            dma((2,)),
            dma((2,)),
            dma((8,)),
            dma((8,)),
            dma((8,)),
            dma((2,)),
            dma((2,)),
            dma((2,)),
            dma((2,)),
            dma((2,)),
            dma((2,)),
            dma((2,)),
            dma((2,)),
            dma((16, 2)),
            dma((16, 2)),
            dma((16,)),
            dma((16,)),
        ],
        compiler_params=pltpu.CompilerParams(
            collective_id=1, has_side_effects=True, vmem_limit_bytes=VMEM_BYTES
        ),
        name="whole",
    )(
        span_order,
        activations,
        noise_mask,
        mask_vector,
        input_weights,
        output_weight,
    )


def solution(mesh):
    in_specs = (P("ctx", None), P("ctx"), P(), P(), P(None, None, "head"), P("head", None))
    out_specs = P(("ctx", "head"), None)
    return jax.shard_map(shards, mesh=mesh, in_specs=in_specs, out_specs=out_specs, check_vma=False)
```

```python
import functools
import math

import jax
import jax.numpy as jnp
from jax import lax
from jax.experimental import pallas as pl
from jax.experimental.pallas import tpu as pltpu
from jax.sharding import PartitionSpec as P

MESH = pl.DeviceIdType.MESH
HEAD = 128
ROWS = 384
HALF = 192
BLOCK = 64
QT = 208
NEG = -1e30
VMEM_BYTES = 60 << 20
NC = 256
LOG2_SCALE = math.log2(math.e) / math.sqrt(HEAD)
F32 = jnp.float32
BF16 = jnp.bfloat16


def coords():
    i = lax.axis_index("ctx")
    j = lax.axis_index("head")
    return j // 2, i // 4, (i // 2) % 2, j % 2, i % 2


def ctx_of(y, zl, c):
    return (y * 2 + zl) * 2 + c


def rcopy(src, dst, ssem, rsem, dev):
    return pltpu.make_async_remote_copy(
        src_ref=src, dst_ref=dst, send_sem=ssem, recv_sem=rsem, device_id=dev, device_id_type=MESH
    )


def greet(devs):
    barrier = pltpu.get_barrier_semaphore()
    for dev in devs:
        pl.semaphore_signal(barrier, inc=1, device_id=dev, device_id_type=MESH)
    return lambda: pl.semaphore_wait(barrier, len(devs))


def kernel(
    span, act, nmask, mvec, w, wo, out,
    lhs, wbuf, st, kv, q, msk, qt, m_ref, o_ref, mc_ref, oc_ref, mn_ref, on_ref, att, abuf, wown, wp, keep, xs, xr, zs, zr,
    act_l, w_l, wo_l, own_l, f_s, f_r, g_r, q_s, q_r, m_s, m_r, zk_s, zf_s, c_s, a_s, a_r,
    wx_s, wx_r, wc_s, wc_r, wy_s, wy_r, wf_s, wf_r, x_s, x_r, z_s, z_r,
):
    x, y, zl, zh, c = coords()
    hd = lax.axis_index("head")
    me = ctx_of(y, zl, c)
    ys = [y] + [lax.rem(y + k, 4) for k in (1, 2, 3)]
    x2 = lax.rem(x + 2, 4)
    ydev = [(ctx_of(ys[k], zl, c), hd) for k in range(4)]
    adev = [ydev, [(ctx_of(ys[k], zl, c), x2 * 2 + zh) for k in range(4)]]
    zdev = (ctx_of(y, 1 - zl, c), hd)
    ddev = (ctx_of(ys[2], 1 - zl, c), hd)
    cdev = (ctx_of(y, zl, 1 - c), hd)
    xup = (me, lax.rem(x + 1, 4) * 2 + zh)
    xdn = (me, lax.rem(x + 3, 4) * 2 + zh)
    hdev = (me, x * 2 + 1 - zh)
    wydev = (ctx_of(lax.rem(y + 1 + 2 * c, 4), zl, c), hd)
    arrive = greet(ydev[1:] + adev[1] + [zdev, ddev, cdev, xup, xdn, hdev])

    sends = []

    def start(cp):
        cp.start()
        sends.append(cp)

    loads = []
    for kc in range(4):
        part = pl.ds(kc * 1024, 1024)
        loads.append(
            (
                pltpu.make_async_copy(act.at[:, part], lhs.at[pl.ds(0, ROWS), part], act_l.at[kc]),
                pltpu.make_async_copy(w.at[0, part], wbuf.at[0, part], w_l.at[kc]),
            )
        )
    wk = pltpu.make_async_copy(w.at[1], wbuf.at[1], w_l.at[4])
    wv = pltpu.make_async_copy(w.at[2], wbuf.at[2], w_l.at[5])
    qd = lax.rem(y, 2) * 2 + c
    order = (qd, qd + 1 - 2 * c, lax.rem(qd + 2, 4), lax.rem(qd + 2, 4) + 1 - 2 * c)
    wol = []
    for n in range(4):
        col = pl.multiple_of(order[n] * 1024, 1024)
        wol.append(pltpu.make_async_copy(wo.at[:, pl.ds(col, 1024)], wown.at[n], wo_l.at[n]))

    def load(*copies):
        for cp in copies:
            cp.start()

    load(*loads[0], *loads[1], *loads[2])
    lhs[pl.ds(ROWS, 16), :] = jnp.broadcast_to(mvec[...].reshape(1, 4096), (16, 4096))
    msk[y] = jnp.broadcast_to(nmask[...].astype(F32).reshape(1, ROWS), (8, ROWS))

    def keep_heads(m, r):
        for j in range(4):
            st[m, j] = r[:, j * HEAD : (j + 1) * HEAD].astype(BF16)

    arrive()
    for e in range(2):
        col = pl.multiple_of(qd * 1024 + e * 512, 512)
        half = wp.at[0, :, pl.ds(e * 512, 512)]
        start(rcopy(wo.at[:, pl.ds(col, 512)], half, wx_s.at[e], wx_r.at[e], adev[1][0]))

    rows = pl.ds(0, ROWS)
    r = None
    for kc in range(4):
        for cp in loads[kc]:
            cp.wait()
        if kc == 0:
            load(*loads[3])
        if kc == 1:
            load(wk)
        part = pl.ds(kc * 1024, 1024)
        d = jnp.dot(lhs[:, part], wbuf[0, part], preferred_element_type=F32)
        r = d if r is None else r + d
    load(wv)
    keep_heads(0, r * LOG2_SCALE)
    for k in (1, 3, 2):
        start(rcopy(st.at[0, ys[k], rows], q.at[y], q_s.at[k], q_r.at[y], ydev[k]))
        start(rcopy(msk.at[y], msk.at[y], m_s.at[k], m_r.at[y], ydev[k]))
    q[y] = st[0, y, rows]

    for m, cp in ((1, wk), (2, wv)):
        cp.wait()
        if m == 2:
            load(*wol)
        keep_heads(m, jnp.dot(lhs[...], wbuf[m], preferred_element_type=F32))
        dst = kv.at[me, m - 1]
        start(rcopy(st.at[m, y, rows], dst, zk_s.at[m - 1], f_r.at[m - 1, me], zdev))
        for k in (1, 3):
            start(rcopy(st.at[m, ys[k], rows], dst, f_s.at[m - 1, k], f_r.at[m - 1, me], ydev[k]))
        kv[me, m - 1] = st[m, y, rows]
    start(rcopy(kv.at[me], kv.at[me], c_s.at[0], g_r.at[me], cdev))
    for m in (1, 2):
        dst = kv.at[me, m - 1]
        start(rcopy(st.at[m, ys[2], rows], dst, f_s.at[m - 1, 2], f_r.at[m - 1, me], ydev[2]))
        start(rcopy(st.at[m, ys[2], rows], dst, f_s.at[m - 1, 0], f_r.at[m - 1, me], ddev))
    def here(k, z, split):
        slot = ctx_of(ys[k], z, c)
        if split:
            for m in range(2):
                rcopy(kv.at[slot, m], kv.at[slot, m], zk_s.at[m], f_r.at[m, slot], cdev).wait_recv()
        else:
            rcopy(kv.at[slot], kv.at[slot], zk_s.at[0], g_r.at[slot], cdev).wait_recv()
        return slot

    def to_core(n, slot):
        start(rcopy(kv.at[slot], kv.at[slot], c_s.at[n], g_r.at[slot], cdev))

    def to_z(n, slot):
        start(rcopy(kv.at[slot], kv.at[slot], zf_s.at[n], g_r.at[slot], zdev))

    def from_core(k, z):
        slot = ctx_of(ys[k], z, 1 - c)
        rcopy(kv.at[slot], kv.at[slot], zk_s.at[0], g_r.at[slot], cdev).wait_recv()

    def send_wp(e):
        half = wp.at[0, :, pl.ds(e * 512, 512)]
        rcopy(half, half, wx_s.at[e], wx_r.at[e], cdev).wait_recv()
        start(rcopy(half, wp.at[1, :, pl.ds(e * 512, 512)], wc_s.at[e], wc_r.at[e], cdev))
        start(rcopy(half, wp.at[2, :, pl.ds(e * 512, 512)], wy_s.at[e], wy_r.at[e], wydev))

    def chunk(pa, pb):
        place = lax.broadcasted_iota(jnp.int32, (1, 4 * ROWS), 1) // HALF
        ks = jnp.zeros((1, 4 * ROWS), jnp.int32)
        for n in range(8):
            ks = jnp.where(place == n, span[4 * (pa if n < 4 else pb) + n % 4], ks)
        refs = [(p, m) for m in range(2) for p in (pa, pb)]
        got = [kv[pl.ds(2 * p, 2), m].reshape(2 * ROWS, HEAD) for p, m in refs]
        k = jnp.concatenate(got[:2], axis=0)
        v = jnp.concatenate(got[2:], axis=0)
        return k, jnp.concatenate([v, jnp.ones((4 * ROWS, HEAD), BF16)], axis=1), ks

    def attend(i, u, keys, first):
        k, v, ks = keys
        sc = lax.dot_general(qt[i], k, (((1,), (1,)), ((), ())), preferred_element_type=F32)
        sc = sc + jnp.where(ks < u, F32(0), F32(NEG))
        top = jnp.max(sc, axis=1, keepdims=True)
        if first:
            new = jnp.maximum(top, F32(NEG))
        else:
            old = m_ref[i][:, :1]
            new = jnp.maximum(old, top)
        p = jnp.exp2(sc - new).astype(BF16)
        o = jnp.dot(p, v, preferred_element_type=F32)
        if not first:
            o = o_ref[i] * jnp.exp2(old - new) + o
        return new, o

    def step(pa, pb, first):
        keys = chunk(pa, pb)
        for i in range(8):
            u = span[2 * ctx_of(i // 2, zl, c) + i % 2]
            new, o = attend(i, u, keys, first)
            m_ref[i] = jnp.broadcast_to(new, (QT, HEAD))
            o_ref[i] = o

    def pair(k, z):
        return ys[k] * 2 + z

    p_x = x // 2
    rowi = lax.broadcasted_iota(jnp.int32, (QT, HALF), 0)
    coli = lax.broadcasted_iota(jnp.int32, (QT, HALF), 1)
    bi = jnp.where(rowi < HALF, rowi // BLOCK, jnp.minimum(rowi - HALF, 2))
    bj = coli // BLOCK

    def own_keys(s):
        km = st[1, y, pl.ds(ROWS, 16), :]
        vm = st[2, y, pl.ds(ROWS, 16), :][:1].astype(F32)
        vm = jnp.concatenate([vm, jnp.ones((1, HEAD), F32)], axis=1)
        src = ctx_of(s, zl, c)
        for h in range(2):
            i = 2 * s + h
            qi = jnp.concatenate([q[s, pl.ds(h * HALF, HALF), :], st[0, y, pl.ds(ROWS, 16), :]], axis=0)
            ko = kv[src, 0, pl.ds(h * HALF, HALF), :]
            vo = kv[src, 1, pl.ds(h * HALF, HALF), :]
            vo = jnp.concatenate([vo, jnp.ones((HALF, HEAD), BF16)], axis=1)
            so = lax.dot_general(qi, ko, (((1,), (1,)), ((), ())), preferred_element_type=F32)
            sm = lax.dot_general(qi, km, (((1,), (1,)), ((), ())), preferred_element_type=F32)[:, :1]
            mrow = msk[s, pl.ds(0, 1), pl.ds(h * HALF, HALF)]
            sc = jnp.where(bj <= bi, so, F32(NEG))
            mc = jnp.max(sc, axis=1, keepdims=True)
            pc = jnp.exp2(sc - mc).astype(BF16)
            mc_ref[i] = jnp.broadcast_to(mc, (QT, HEAD))
            oc_ref[i] = jnp.dot(pc, vo, preferred_element_type=F32)
            hit = (bj == bi) & (mrow > 0.5)
            sn = jnp.where(hit, sm, sc)
            mn = jnp.max(sn, axis=1, keepdims=True)
            pn = jnp.exp2(sn - mn).astype(BF16).astype(F32)
            pz = jnp.where(hit, F32(0), pn)
            wm = jnp.sum(pn - pz, axis=1, keepdims=True)
            mn_ref[i] = jnp.broadcast_to(mn, (QT, HEAD))
            on_ref[i] = jnp.dot(pz.astype(BF16), vo, preferred_element_type=F32) + wm * vm

    for h in range(2):
        qt[2 * y + h, pl.ds(0, HALF), :] = q[y, pl.ds(h * HALF, HALF), :]
        qt[2 * y + h, pl.ds(HALF, 16), :] = st[0, y, pl.ds(ROWS, 16), :]
    own_keys(y)
    to_core(1, here(0, 1 - zl, True))
    for n, k in ((0, 1), (1, 3)):
        slot = here(k, zl, True)
        to_z(n, slot)
        to_core(2 + n, slot)
    for k in (1, 3, 2):
        rcopy(q.at[ys[k]], q.at[ys[k]], q_s.at[1], q_r.at[ys[k]], cdev).wait_recv()
        rcopy(msk.at[ys[k]], msk.at[ys[k]], m_s.at[1], m_r.at[ys[k]], cdev).wait_recv()
    for k in (1, 3, 2):
        for h in range(2):
            qt[2 * ys[k] + h, pl.ds(0, HALF), :] = q[ys[k], pl.ds(h * HALF, HALF), :]
            qt[2 * ys[k] + h, pl.ds(HALF, 16), :] = st[0, y, pl.ds(ROWS, 16), :]
    from_core(0, zl)
    from_core(0, 1 - zl)
    step(pair(0, zl), pair(0, 1 - zl), True)
    own_keys(ys[1])
    own_keys(ys[3])
    from_core(1, zl)
    from_core(3, zl)
    step(pair(1, zl), pair(3, zl), False)
    to_core(4, here(2, zl, True))
    to_core(5, here(1, 1 - zl, False))
    send_wp(0)
    own_keys(ys[2])
    from_core(2, zl)
    from_core(1, 1 - zl)
    step(pair(2, zl), pair(1, 1 - zl), False)
    to_core(6, here(3, 1 - zl, False))
    to_core(7, here(2, 1 - zl, True))
    send_wp(1)
    from_core(3, 1 - zl)
    from_core(2, 1 - zl)

    def join(mp, op, mo, oo):
        top = jnp.maximum(mp, mo)
        o = op * jnp.exp2(mp - top) + oo * jnp.exp2(mo - top)
        return o[:, :HEAD] / o[:, HEAD:]

    def finish(s, h, mp, op):
        i = 2 * s + h
        mrow = msk[s, pl.ds(0, 1), pl.ds(h * HALF, HALF)]
        clean = join(mp, op, mc_ref[i][:, :1], oc_ref[i])[:HALF].astype(BF16)
        an = join(mp, op, mn_ref[i][:, :1], on_ref[i])
        mcol = jnp.sum(jnp.where(rowi == coli, mrow, F32(0)), axis=1, keepdims=True)[:HALF]
        masked = jnp.concatenate(
            [jnp.broadcast_to(an[HALF + b : HALF + b + 1], (BLOCK, HEAD)) for b in range(3)], axis=0
        )
        noisy = jnp.where(mcol > 0.5, masked, an[:HALF]).astype(BF16)

        for b in range(4):
            xo = 2 * h + b // 2
            zo = b % 2
            near = zo == p_x
            side = jnp.where(near, lax.rem(x + 1, 4), lax.rem(x + 3, 4))
            pos = jnp.where(
                xo == x,
                zo,
                jnp.where(xo == x2, 4 + zo, jnp.where(near, 0, 4) + jnp.where(xo == side, 2, 3)),
            )
            att[s, pos, pl.ds(0, 48), :] = clean[b * 48 : (b + 1) * 48]
            att[s, pos, pl.ds(48, 48), :] = noisy[b * 48 : (b + 1) * 48]

    last = chunk(pair(3, 1 - zl), pair(2, 1 - zl))
    own = None
    for group in ((2, 1), (3, 0)):
        done = [
            [attend(2 * ys[k] + h, span[2 * ctx_of(ys[k], zl, c) + h], last, False) for h in range(2)]
            for k in group
        ]
        for k, parts in zip(group, done):
            s = ys[k]
            for h in range(2):
                finish(s, h, *parts[h])
            for t in (1, 0):
                dst = abuf.at[:, :, pl.ds(pl.multiple_of((4 * t + y) * HEAD, HEAD), HEAD)]
                if (t, k) == (0, 0):
                    own = pltpu.make_async_copy(att.at[s, pl.ds(0, 4)], dst, own_l)
                    own.start()
                else:
                    start(
                        rcopy(att.at[s, pl.ds(4 * t, 4)], dst, a_s.at[4 * t + k], a_r.at[4 * t + y], adev[t][k])
                    )
    own.wait()
    for t, k in ((0, 2), (1, 2), (0, 1), (1, 1), (0, 3), (1, 3), (1, 0)):
        slot = 4 * t + ys[k]
        dst = abuf.at[:, :, pl.ds(pl.multiple_of(slot * HEAD, HEAD), HEAD)]
        rcopy(att.at[0, pl.ds(0, 4)], dst, a_s.at[1], a_r.at[slot], cdev).wait_recv()

    def matmul(n):
        j, e = n // 4, n // 2 % 2
        if n % 4 == 0:
            wol[j].wait()
        half = wp.at[j, :, pl.ds(e * 512, 512)]
        if n % 2 == 0 and j == 1:
            rcopy(half, half, wc_s.at[e], wc_r.at[e], cdev).wait_recv()
        if n % 2 == 0 and j == 2:
            rcopy(half, half, wy_s.at[e], wy_r.at[e], cdev).wait_recv()
            start(rcopy(half, wp.at[3, :, pl.ds(e * 512, 512)], wf_s.at[e], wf_r.at[e], cdev))
        if n % 2 == 0 and j == 3:
            rcopy(half, half, wf_s.at[e], wf_r.at[e], cdev).wait_recv()
        cols = pl.ds(n % 4 * NC, NC)
        a = abuf[...].reshape(ROWS, 1024)
        r = jnp.dot(a[:, :512], wown[j, :, cols], preferred_element_type=F32)
        r = r + jnp.dot(a[:, 512:], wp[j, :, cols], preferred_element_type=F32)
        keep[n] = r[:192].reshape(2, 96, NC)
        xs[n, 0] = r[192:288].astype(BF16)
        xs[n, 1] = r[288:].astype(BF16)
        start(rcopy(xs.at[n, 0], xr.at[n, 0], x_s.at[n, 0], x_r.at[n, 0], xup))
        start(rcopy(xs.at[n, 1], xr.at[n, 1], x_s.at[n, 1], x_r.at[n, 1], xdn))

    from_below = lax.rem(x + 3, 4) // 2

    def reduce_x(n):
        for d in range(2):
            rcopy(xs.at[n, d], xr.at[n, d], x_s.at[n, d], x_r.at[n, d], xup).wait_recv()
        far = 1 - zh
        keep[n, zh] = keep[n, zh] + xr[n, (zh + from_below) % 2].astype(F32)
        zs[n] = (keep[n, far] + xr[n, (far + from_below) % 2].astype(F32)).astype(BF16)
        start(rcopy(zs.at[n], zr.at[n], z_s.at[n], z_r.at[n], hdev))

    def reduce_z(n):
        rcopy(zs.at[n], zr.at[n], z_s.at[n], z_r.at[n], hdev).wait_recv()
        total = (keep[n, zh] + zr[n].astype(F32)).astype(BF16)
        col = pl.multiple_of(order[n // 4] * 1024 + n % 4 * NC, NC)
        out[:, pl.ds(col, NC)] = total[:48]
        out[:, pl.ds(4096 + col, NC)] = total[48:]

    for n in range(8):
        matmul(n)
    for n in range(16):
        reduce_x(n)
        if n + 8 < 16:
            matmul(n + 8)
        if n >= 6:
            reduce_z(n - 6)
    for n in range(10, 16):
        reduce_z(n)
    for cp in sends:
        cp.wait_send()


def vmem():
    return pl.BlockSpec(memory_space=pltpu.VMEM)


def anyspace():
    return pl.BlockSpec(memory_space=pl.ANY)


def shards(activations, noise_mask, span_order, mask_vector, input_weights, output_weight):
    dma = pltpu.SemaphoreType.DMA
    return pl.pallas_call(
        kernel,
        out_shape=jax.ShapeDtypeStruct((48, 8192), BF16),
        in_specs=[pl.BlockSpec(memory_space=pltpu.SMEM), anyspace(), vmem(), vmem(), anyspace(), anyspace()],
        out_specs=vmem(),
        scratch_shapes=[
            pltpu.VMEM((ROWS + 16, 4096), BF16),
            pltpu.VMEM((3, 4096, 512), BF16),
            pltpu.VMEM((3, 4, ROWS + 16, HEAD), BF16),
            pltpu.VMEM((16, 2, ROWS, HEAD), BF16),
            pltpu.VMEM((4, ROWS, HEAD), BF16),
            pltpu.VMEM((4, 8, ROWS), F32),
            pltpu.VMEM((8, QT, HEAD), BF16),
            pltpu.VMEM((8, QT, HEAD), F32),
            pltpu.VMEM((8, QT, 2 * HEAD), F32),
            pltpu.VMEM((8, QT, HEAD), F32),
            pltpu.VMEM((8, QT, 2 * HEAD), F32),
            pltpu.VMEM((8, QT, HEAD), F32),
            pltpu.VMEM((8, QT, 2 * HEAD), F32),
            pltpu.VMEM((4, 8, 96, HEAD), BF16),
            pltpu.VMEM((4, 96, 1024), BF16),
            pltpu.VMEM((4, 512, 1024), BF16),
            pltpu.VMEM((4, 512, 1024), BF16),
            pltpu.VMEM((16, 2, 96, NC), F32),
            pltpu.VMEM((16, 2, 96, NC), BF16),
            pltpu.VMEM((16, 2, 96, NC), BF16),
            pltpu.VMEM((16, 96, NC), BF16),
            pltpu.VMEM((16, 96, NC), BF16),
            dma((4,)),
            dma((6,)),
            dma((4,)),
            dma,
            dma((2, 4)),
            dma((2, 16)),
            dma((16,)),
            dma((4,)),
            dma((4,)),
            dma((4,)),
            dma((4,)),
            dma((2,)),
            dma((2,)),
            dma((8,)),
            dma((8,)),
            dma((8,)),
            dma((2,)),
            dma((2,)),
            dma((2,)),
            dma((2,)),
            dma((2,)),
            dma((2,)),
            dma((2,)),
            dma((2,)),
            dma((16, 2)),
            dma((16, 2)),
            dma((16,)),
            dma((16,)),
        ],
        compiler_params=pltpu.CompilerParams(
            collective_id=1, has_side_effects=True, vmem_limit_bytes=VMEM_BYTES
        ),
        name="whole",
    )(
        span_order,
        activations,
        noise_mask,
        mask_vector,
        input_weights,
        output_weight,
    )


def solution(mesh):
    in_specs = (P("ctx", None), P("ctx"), P(), P(), P(None, None, "head"), P("head", None))
    out_specs = P(("ctx", "head"), None)
    return jax.shard_map(shards, mesh=mesh, in_specs=in_specs, out_specs=out_specs, check_vma=False)
```
